128 devices in a mesh: lon: 32 (over z_hi, y, x), lat: 4 (over z_lo, core).
Axes of the slice: x: 4, y: 4, z: 4 (z_hi: 2, z_lo: 2; z = z_hi * 2 + z_lo), core: 2. Of those that a mesh axis runs over, the one named last changes fastest.
Arguments:
- tokens: bfloat16 [4, 48, 384, 512], P(None, 'lat', 'lon'), may hold values from -6 to 6
- grad_output: bfloat16 [4, 48, 384, 512], P(None, 'lat', 'lon'), may hold values from -6 to 6
- norm_gain: float32 [512], replicated, may hold values from 0.1 to 1.9
- norm_bias: float32 [512], replicated, may hold values from -3 to 3
- w_qkv: bfloat16 [512, 1536], replicated, may hold values from -0.25 to 0.25
- w_proj: bfloat16 [512, 512], replicated, may hold values from -0.25 to 0.25
- rel_bias: float32 [8, 759], replicated, may hold values from -3 to 246
Outputs:
- grad_tokens: bfloat16 [4, 48, 384, 512], P(None, 'lat', 'lon')
- grad_qkv_weight: float32 [512, 1536], replicated
- grad_proj_weight: float32 [512, 512], replicated
- grad_norm_gain: float32 [512], replicated
- grad_norm_bias: float32 [512], replicated
- grad_rel_bias: float32 [8, 759], replicated
The draws below stay inside these ranges and needn't reach their ends.
All inputs are finite; a program needn't handle non-finite values.
Results may differ from the reference program's by a relative error of at most 0.014.
Values may be sent and summed in bfloat16 or wider, within the bound.
A program may use at most 128 MiB of HBM per device.

```python
import math
import jax
import jax.numpy as jnp
from jax import lax

D = 512
HEADS = 8
WIN_LEV = 2
WIN_LAT = 6
WIN_LON = 12
LEVELS = 4
NLAT = 48
NLON = 384
TOKENS = 73728
RELS = 759


def draw_rel_bias(key, part):
    key = jax.random.fold_in(key, 11)
    key_base = jax.random.fold_in(key, 0)
    base = jnp.clip(jax.random.normal(key_base, (HEADS, RELS), jnp.float32), -3.0, 3.0)
    return base


def steps_of(own_key, shape, cuts, low, largest):
    def one(axis_at, shards_of):
        steps = jax.random.uniform(jax.random.fold_in(jax.random.fold_in(own_key, 6), axis_at), (shards_of,), jnp.float32, low / len(cuts), largest / len(cuts))
        return jnp.repeat(jnp.exp(steps), shape[axis_at] // shards_of).reshape((-1,) + (1,) * (len(shape) - axis_at - 1))

    factor_of = one(*cuts[0])
    for cut in cuts[1:]:
        factor_of = factor_of * one(*cut)
    return factor_of


def noise(stream_key, dims, width, reach, pieces=(), kind=jnp.bfloat16):
    values = jax.random.normal(stream_key, dims, jnp.float32) * width
    if len(pieces) > 0:
        values = steps_of(stream_key, dims, pieces, -0.22, 0.18) * values
    return jnp.clip(values, min=-reach, max=reach).astype(kind)


def setup_inputs(seed: int = 0) -> dict:
    seeds = jax.random.split(jax.random.key(seed), 8)
    tokens = noise(seeds[0], (LEVELS, NLAT, NLON, D), 1.0, 6.0, ((1, 4), (2, 32)))
    grad_output = noise(seeds[1], (LEVELS, NLAT, NLON, D), 1.0, 6.0, ((1, 4), (2, 32)))
    norm_gain = jnp.clip(1.0 + 0.18 * jax.random.normal(seeds[2], (D,), jnp.float32), 0.1, 1.9)
    norm_bias = noise(seeds[3], (D,), 0.5, 3.0, (), jnp.float32)
    w_qkv = noise(seeds[4], (D, 3 * D), D ** -0.5, 0.25)
    w_proj = noise(seeds[5], (D, D), D ** -0.5, 0.25)
    rel_bias = draw_rel_bias(jax.random.fold_in(seeds[7], 71), 0)
    return dict(tokens=tokens, grad_output=grad_output, norm_gain=norm_gain, norm_bias=norm_bias, w_qkv=w_qkv, w_proj=w_proj, rel_bias=rel_bias)


norm_eps = 1e-05
masked_score = -1000000000.0

def one_hots(extent):
    positions = jnp.arange(extent, dtype=jnp.int32)
    offsets = jnp.arange(2 * extent - 1, dtype=jnp.int32)
    return (positions[None, :, None] - positions[:, None, None] + extent - 1 == offsets[None, None, :]).astype(jnp.float32)

def to_windows(array, win_lev, win_lat, win_lon):
    levels, rows, cols, last_dim = array.shape
    shaped = array.reshape(levels // win_lev, win_lev, rows // win_lat, win_lat, cols // win_lon, win_lon, last_dim)
    return shaped.transpose(0, 2, 4, 1, 3, 5, 6).reshape(-1, win_lev * win_lat * win_lon, last_dim)

def from_windows(array, levels, rows, cols, win_lev, win_lat, win_lon):
    last_dim = array.shape[-1]
    shaped = array.reshape(levels // win_lev, rows // win_lat, cols // win_lon, win_lev, win_lat, win_lon, last_dim)
    return shaped.transpose(0, 3, 1, 4, 2, 5, 6).reshape(levels, rows, cols, last_dim)

def window_backward(x_win, g_win, region, norm_gain, norm_bias, w_qkv, w_proj, rel_bias, win_lev, win_lat, win_lon):
    win_count, tok_win, model_width = x_win.shape
    head_count = rel_bias.shape[0]
    head_dim = model_width // head_count
    score_scale = 1.0 / math.sqrt(head_dim)
    hp = lax.Precision.HIGHEST
    x_full = x_win.astype(jnp.float32)
    average = lax.optimization_barrier(jnp.mean(x_full, -1, keepdims=True))
    centred = x_full - average
    variance = lax.optimization_barrier(jnp.mean(centred * centred, -1, keepdims=True))
    inv_std = lax.rsqrt(variance + norm_eps)
    x_hat = centred * inv_std
    normed = (x_hat * norm_gain + norm_bias).astype(jnp.bfloat16)
    flat_in = normed.reshape(win_count * tok_win, model_width)
    qkv_all = jnp.dot(flat_in, w_qkv, preferred_element_type=jnp.float32).astype(jnp.bfloat16)
    qkv_all = qkv_all.reshape(win_count, tok_win, 3, head_count, head_dim)
    query_h = qkv_all[:, :, 0].astype(jnp.float32)
    key_h = qkv_all[:, :, 1].astype(jnp.float32)
    value_h = qkv_all[:, :, 2].astype(jnp.float32)
    hot_lev = one_hots(win_lev)
    hot_lat = one_hots(win_lat)
    hot_lon = one_hots(win_lon)
    bias_table = rel_bias.reshape(head_count, 2 * win_lev - 1, 2 * win_lat - 1, 2 * win_lon - 1)
    bias_full = jnp.einsum('hxyz,psx,qty,ruz->hpqrstu', bias_table, hot_lev, hot_lat, hot_lon, precision=hp)
    bias_full = bias_full.reshape(head_count, tok_win, tok_win)
    scores = jnp.einsum('bihc,bjhc->bhij', query_h, key_h) * score_scale + bias_full
    allowed = region[:, None, :, None] == region[:, None, None, :]
    scores = jnp.where(allowed, scores, masked_score)
    row_max = lax.optimization_barrier(jnp.max(scores, -1, keepdims=True))
    exp_scores = jnp.exp(scores - row_max)
    probs = exp_scores / lax.optimization_barrier(jnp.sum(exp_scores, -1, keepdims=True))
    probs_b = probs.astype(jnp.bfloat16)
    attended = jnp.einsum('bhij,bjhc->bihc', probs_b.astype(jnp.float32), value_h).astype(jnp.bfloat16)
    attended = attended.reshape(win_count * tok_win, model_width)
    grad_flat = g_win.reshape(win_count * tok_win, model_width)
    d_proj = jnp.dot(attended.T, grad_flat, preferred_element_type=jnp.float32)
    g_att = jnp.dot(grad_flat, w_proj.T, preferred_element_type=jnp.float32).astype(jnp.bfloat16)
    g_att = g_att.reshape(win_count, tok_win, head_count, head_dim).astype(jnp.float32)
    d_probs = jnp.einsum('bihc,bjhc->bhij', g_att, value_h)
    d_value = jnp.einsum('bhij,bihc->bjhc', probs_b.astype(jnp.float32), g_att).astype(jnp.bfloat16)
    d_scores = probs * (d_probs - lax.optimization_barrier(jnp.sum(probs * d_probs, -1, keepdims=True)))
    d_bias_sum = lax.optimization_barrier(jnp.sum(d_scores, 0)).reshape(head_count, win_lev, win_lat, win_lon, win_lev, win_lat, win_lon)
    d_table = jnp.einsum('hpqrstu,psx,qty,ruz->hxyz', d_bias_sum, hot_lev, hot_lat, hot_lon, precision=hp)
    d_scaled = (d_scores * score_scale).astype(jnp.bfloat16).astype(jnp.float32)
    d_query = jnp.einsum('bhij,bjhc->bihc', d_scaled, key_h).astype(jnp.bfloat16)
    d_key = jnp.einsum('bhij,bihc->bjhc', d_scaled, query_h).astype(jnp.bfloat16)
    d_qkv = jnp.stack([d_query, d_key, d_value], 2).reshape(win_count * tok_win, 3 * model_width)
    d_wqkv = jnp.dot(flat_in.T, d_qkv, preferred_element_type=jnp.float32)
    d_normed = jnp.dot(d_qkv, w_qkv.T, preferred_element_type=jnp.float32).reshape(win_count, tok_win, model_width)
    d_gain = lax.optimization_barrier(jnp.sum(d_normed * x_hat, (0, 1)))
    d_beta = lax.optimization_barrier(jnp.sum(d_normed, (0, 1)))
    g_hat = d_normed * norm_gain
    d_branch = inv_std * (g_hat - lax.optimization_barrier(jnp.mean(g_hat, -1, keepdims=True)) - x_hat * lax.optimization_barrier(jnp.mean(g_hat * x_hat, -1, keepdims=True)))
    return (d_branch.astype(jnp.bfloat16), (d_wqkv, d_proj, d_gain, d_beta, d_table.reshape(head_count, -1)))

def reference(tokens, grad_output, norm_gain, norm_bias, w_qkv, w_proj, rel_bias):
    levels, rows, cols, model_width = tokens.shape
    half_lev, half_lat, half_lon = (WIN_LEV // 2, WIN_LAT // 2, WIN_LON // 2)
    shifted_in = jnp.roll(tokens, (-half_lev, -half_lat, -half_lon), (0, 1, 2))
    shifted_grad = jnp.roll(grad_output, (-half_lev, -half_lat, -half_lon), (0, 1, 2))
    lev_wrap = ((jnp.arange(levels, dtype=jnp.int32) + half_lev) % levels < half_lev).astype(jnp.int32)
    lat_wrap = ((jnp.arange(rows, dtype=jnp.int32) + half_lat) % rows < half_lat).astype(jnp.int32)
    region = jnp.broadcast_to(lev_wrap[:, None, None] * 2 + lat_wrap[None, :, None], (levels, rows, cols))
    x_windows = to_windows(shifted_in, WIN_LEV, WIN_LAT, WIN_LON)
    g_windows = to_windows(shifted_grad, WIN_LEV, WIN_LAT, WIN_LON)
    r_windows = to_windows(region[..., None], WIN_LEV, WIN_LAT, WIN_LON)[..., 0]
    win_total, tok_win = r_windows.shape
    batch = math.gcd(win_total, 16)
    steps_count = win_total // batch
    x_batches = x_windows.reshape(steps_count, batch, tok_win, model_width)
    g_batches = g_windows.reshape(steps_count, batch, tok_win, model_width)
    r_batches = r_windows.reshape(steps_count, batch, tok_win)
    zeros_init = (jnp.zeros((model_width, 3 * model_width), jnp.float32), jnp.zeros((model_width, model_width), jnp.float32), jnp.zeros((model_width,), jnp.float32), jnp.zeros((model_width,), jnp.float32), jnp.zeros(rel_bias.shape, jnp.float32))

    def one_batch(carry, inputs):
        x_batch, g_batch, r_batch = inputs
        d_branch, grads = window_backward(x_batch, g_batch, r_batch, norm_gain, norm_bias, w_qkv, w_proj, rel_bias, WIN_LEV, WIN_LAT, WIN_LON)
        return (tuple((c + g for c, g in zip(carry, grads))), d_branch)
    totals, branches = lax.scan(one_batch, zeros_init, (x_batches, g_batches, r_batches))
    branch_grid = from_windows(branches.reshape(win_total, tok_win, model_width), levels, rows, cols, WIN_LEV, WIN_LAT, WIN_LON)
    rolled_back = jnp.roll(branch_grid, (half_lev, half_lat, half_lon), (0, 1, 2))
    grad_tokens = (grad_output.astype(jnp.float32) + rolled_back.astype(jnp.float32)).astype(jnp.bfloat16)
    factor = TOKENS ** (-0.5)
    d_wqkv, d_proj, d_gain, d_beta, d_table = totals
    return (grad_tokens, d_wqkv * factor, d_proj * factor, d_gain * factor, d_beta * factor, d_table * factor)
```

```python
import functools

import jax
import jax.numpy as jnp
from jax import lax
from jax.experimental import pallas as pl
from jax.experimental.pallas import tpu as pltpu
from jax.sharding import PartitionSpec as P

F32 = jnp.float32
BF16 = jnp.bfloat16
MESH = pl.DeviceIdType.MESH

NT = 144
WINS = 4
TOK = WINS * NT
D = 512
HEADS = 8
PAIRS = 4
RELS = 759
EPS = 1e-5
MASKED = -1e9
FACTOR = 73728 ** (-0.5)

PIECES = {
    "A": (0, 108, 112, 0, -1),
    "B": (112, 36, 48, -1, -1),
    "C": (160, 72, 80, -1, 0),
    "D": (240, 108, 112, 0, 1),
    "E": (352, 36, 48, -1, 1),
}
SEND_ROWS = 400
PLACES = {
    "A": ((0, 72, 72), (72, 36, 216)),
    "B": ((0, 36, 252),),
    "C": ((0, 36, 180), (36, 36, 540)),
    "D": ((0, 72, 288), (72, 36, 432)),
    "E": ((0, 36, 468),),
}


def half_slab(level, row, half):
    block, lev = {1: (0, 0), 2: (0, 1), 3: (1, 0), 0: (1, 1)}[level]
    off = lev * 18 + (row % 3) * 6
    own = half == 1 - block
    if row < 3:
        if own:
            return False, PIECES["C"][0] + 36 * block + off
        return False, PIECES["B" if block == 0 else "E"][0] + off
    north = (row - 3) // 3 * 36 if row < 9 else 0
    if own:
        return True, (2 * block + (row >= 9)) * NT + 72 * block + north + off
    base = PIECES["A" if block == 0 else "D"][0]
    return False, base + (72 if row >= 9 else north) + off


def place_of(i):
    o6 = i % 6
    a3 = i // 6 % 3
    lev = i // 18 % 2
    ah = i // 36 % 2
    oh = i // 72
    return 253 * lev + 23 * (3 * ah + a3) + 6 * oh + o6


def dot(a, b, precision=None):
    return lax.dot_general(
        a, b, (((1,), (0,)), ((), ())), precision=precision, preferred_element_type=F32
    )


def dot_nt(a, b):
    return lax.dot_general(a, b, (((1,), (1,)), ((), ())), preferred_element_type=F32)


def kernel(
    tok_hbm, grd_hbm, gain_ref, bias_ref, wqkv_hbm, wproj_hbm, rel_ref,
    out_tok, out_wqkv, out_wproj, out_gain, out_beta, out_table,
    tok, grd, wp, wproj, x32, g32, s32, inv, sndx, sndg, rcvx, rcvg, sndr, rcvr,
    normed, normt, qkv, gatt, gwin, dqkv, dn,
    tbl, sh, bj, bias_t, masks, dsum, dproj,
    cb, rc0, b1, rx, b2, ry, b3, rz, gb, ow, op,
    exb, exc, exx, exy, exz,
    load_sem, halo_s, halo_r, ret_s, ret_r, ars, arr, exs, exr, out_sem,
):
    lon = lax.axis_index("lon")
    lat = lax.axis_index("lat")
    core = lat % 2
    zz = (lon // 16) * 2 + lat // 2
    yy = (lon // 4) % 4
    xx = lon % 4

    def chip(z, y, x, c):
        return ((z // 2) * 16 + y * 4 + x, (z % 2) * 2 + c)

    def beside(dlat, dlon):
        return ((lon + dlon + 32) % 32, (lat + dlat + 4) % 4)

    def peer(axis, d):
        if axis == "x":
            return chip(zz, yy, (xx + d) % 4, core)
        if axis == "y":
            return chip(zz, (yy + d) % 4, xx, core)
        return chip((zz + d) % 4, yy, xx, core)

    other = chip(zz, yy, xx, 1 - core)

    barrier = pltpu.get_barrier_semaphore()
    greeted = [beside(a, o) for a in (-1, 0, 1) for o in (-1, 0, 1) if (a, o) != (0, 0)]
    greeted += [other] + [peer(axis, d) for axis in "xyz" for d in (1, 2, 3)]
    for device in greeted:
        pl.semaphore_signal(barrier, inc=1, device_id=device, device_id_type=MESH)

    loads = [
        pltpu.make_async_copy(tok_hbm, tok, load_sem.at[0]),
        pltpu.make_async_copy(grd_hbm, grd, load_sem.at[1]),
        pltpu.make_async_copy(wproj_hbm, wproj, load_sem.at[2]),
    ]
    for p in range(PAIRS):
        for s in range(3):
            loads.append(
                pltpu.make_async_copy(
                    wqkv_hbm.at[:, pl.ds(512 * s + 128 * p, 128)],
                    wp.at[:, pl.ds(384 * p + 128 * s, 128)],
                    load_sem.at[3 + 3 * p + s],
                )
            )
    for copy in loads:
        copy.start()

    def pack(source, mine, first):
        for level in (1, 2, 3, 0):
            for row in range(12):
                slab = source[level, row].astype(F32)
                for half in range(2):
                    own, at = half_slab(level, row, half)
                    piece = slab[6 * half : 6 * half + 6]
                    if own:
                        mine[at : at + 6, :] = piece
                    else:
                        s32[at : at + 6, :] = piece
        first[...] = s32[...].astype(BF16)

    def halo(k, name, src, dst):
        start, _, rows, dlat, dlon = PIECES[name]
        return pltpu.make_async_remote_copy(
            src_ref=src.at[pl.ds(start, rows)],
            dst_ref=dst.at[pl.ds(start, rows)],
            send_sem=halo_s.at[k],
            recv_sem=halo_r.at[k],
            device_id=beside(dlat, dlon),
            device_id_type=MESH,
        )

    xs = [halo(k, name, sndx, rcvx) for k, name in enumerate("ADBEC")]
    gs = [halo(5 + k, name, sndg, rcvg) for k, name in enumerate("ADBEC")]

    s32[...] = jnp.zeros((SEND_ROWS, D), F32)
    loads[0].wait()
    pack(tok, x32, sndx)
    pl.semaphore_wait(barrier, len(greeted))
    for copy in xs:
        copy.start()
    loads[1].wait()
    pack(grd, g32, sndg)
    for copy in gs:
        copy.start()

    tbl[...] = jnp.zeros((HEADS, 768), F32)
    tbl[:, 0:RELS] = rel_ref[...]
    table = tbl[...]
    for j in range(NT):
        at = place_of(j)
        turned = table if at == 0 else pltpu.roll(table, 768 - at, 1)
        sh[8 * j : 8 * j + 8, :] = turned[:, 0:384]

    def picks(shape, dim):
        lane = lax.broadcasted_iota(jnp.int32, shape, 1 - dim)
        place = jnp.where(lane < NT, 379 - place_of(lane), -1)
        return (lax.broadcasted_iota(jnp.int32, shape, dim) == place).astype(F32)

    spread = dot(sh[...], picks((384, 256), 0), lax.Precision.HIGHEST)
    for n in range(2):
        bj[n] = spread[:, 128 * n : 128 * n + 128]
    for h in range(HEADS):
        for n in range(2):
            bias_t[h, :, 128 * n : 128 * n + 128] = bj.at[n][pl.ds(h, NT, stride=8), :]

    ti = lax.broadcasted_iota(jnp.int32, (NT, 256), 0)
    tj = lax.broadcasted_iota(jnp.int32, (NT, 256), 1)
    lev_cut = (ti // 18) % 2 != (tj // 18) % 2
    lat_cut = ((ti // 36) % 2 != (tj // 36) % 2) & (lat == 3)
    masks[0] = jnp.where(lat_cut, MASKED, 0.0)
    masks[1] = jnp.where(lev_cut, MASKED, 0.0)
    masks[2] = jnp.where(lat_cut | lev_cut, MASKED, 0.0)

    def place(copies, source, mine):
        for copy, name in zip(copies, "ADBEC"):
            copy.wait_recv()
            start, _, rows, _, _ = PIECES[name]
            got = source[start : start + rows, :].astype(F32)
            for src, count, dst in PLACES[name]:
                mine[dst : dst + count, :] = got[src : src + count]

    place(xs, rcvx, x32)
    for copy in loads[2:]:
        copy.wait()
    gain = gain_ref[...]
    beta = bias_ref[...]

    def layer_norm(w, _):
        rows = pl.ds(pl.multiple_of(w * NT, NT), NT)
        x = x32[rows, :]
        centred = x - jnp.mean(x, -1, keepdims=True)
        variance = jnp.mean(centred * centred, -1, keepdims=True)
        scale = lax.rsqrt(variance + EPS)
        hat = centred * scale
        x32[rows, :] = hat
        inv[rows, :] = scale
        normed[rows, :] = (hat * gain + beta).astype(BF16)
        return 0

    lax.fori_loop(0, WINS, layer_norm, 0)
    normt[...] = normed[...].T

    def project(n, _):
        cols = pl.ds(pl.multiple_of(n * 256, 256), 256)
        qkv[:, cols] = dot(normed[...], wp[:, cols]).astype(BF16)
        return 0

    lax.fori_loop(0, 6, project, 0)

    place(gs, rcvg, g32)
    gwin[...] = g32[...].astype(BF16)

    def project_g(n, _):
        cols = pl.ds(pl.multiple_of(n * 256, 256), 256)
        gatt[:, cols] = dot_nt(gwin[...], wproj[cols, :]).astype(BF16)
        return 0

    lax.fori_loop(0, 2, project_g, 0)

    def ring(c, sem, axis, src_of, dst_of):
        copies = []
        for d in (1, 2, 3):
            copies.append(
                pltpu.make_async_remote_copy(
                    src_ref=src_of(d),
                    dst_ref=dst_of(d),
                    send_sem=ars.at[c, sem + d - 1],
                    recv_sem=arr.at[c, sem + d - 1],
                    device_id=peer(axis, d),
                    device_id_type=MESH,
                )
            )
        return copies

    def turned_to(at, d):
        return (at + d) % 4

    def rows_at(start, rows):
        return pl.ds(pl.multiple_of(start, 16), rows)

    def phase_copies(c, ph, arriving):
        sign = -1 if arriving else 1
        if ph in (0, 7):
            if ph == 0:
                src = cb.at[c, rows_at((1 - core) * 1024, 1024)]
                dst = rc0.at[c]
            else:
                src = gb.at[c, rows_at(core * 1024, 1024)]
                dst = gb.at[c, rows_at((1 - core if arriving else core) * 1024, 1024)]
            k = 0 if ph == 0 else 19
            return [
                pltpu.make_async_remote_copy(
                    src_ref=src, dst_ref=dst, send_sem=ars.at[c, k], recv_sem=arr.at[c, k],
                    device_id=other, device_id_type=MESH,
                )
            ]
        if ph == 1:
            return ring(c, 1, "x", lambda d: b1.at[c, rows_at(turned_to(xx, d) * 256, 256)], lambda d: rx.at[c, d - 1])
        if ph == 2:
            return ring(c, 4, "y", lambda d: b2.at[c, rows_at(turned_to(yy, d) * 64, 64)], lambda d: ry.at[c, d - 1])
        if ph == 3:
            return ring(c, 7, "z", lambda d: b3.at[c, rows_at(turned_to(zz, d) * 16, 16)], lambda d: rz.at[c, d - 1])

        def span(d):
            half = core * 1024
            x = xx if ph < 6 else (xx + d + 4) % 4
            y = yy if ph != 5 else (yy + d + 4) % 4
            z = zz if ph != 4 else (zz + d + 4) % 4
            if ph == 4:
                return rows_at(half + x * 256 + y * 64 + z * 16, 16)
            if ph == 5:
                return rows_at(half + x * 256 + y * 64, 64)
            return rows_at(half + x * 256, 256)

        axis = {4: "z", 5: "y", 6: "x"}[ph]
        sem = {4: 10, 5: 13, 6: 16}[ph]
        return ring(c, sem, axis, lambda d: gb.at[c, span(0)], lambda d: gb.at[c, span(-d if arriving else 0)])

    def send(c, ph):
        for copy in phase_copies(c, ph, False):
            copy.start()

    def receive(c, ph):
        for copy in phase_copies(c, ph, True):
            copy.wait_recv()
        if ph == 0:
            own = cb[c, rows_at(core * 1024, 1024), :].astype(F32)
            b1[c] = (own + rc0[c].astype(F32)).astype(BF16)
        elif ph in (1, 2, 3):
            src, got, at, rows = {1: (b1, rx, xx, 256), 2: (b2, ry, yy, 64), 3: (b3, rz, zz, 16)}[ph]
            own = src[c, rows_at(at * rows, rows), :].astype(F32)
            for d in range(3):
                own = own + got[c, d].astype(F32)
            own = own.astype(BF16)
            if ph == 1:
                b2[c] = own
            elif ph == 2:
                b3[c] = own
            else:
                gb[c, rows_at(core * 1024 + xx * 256 + yy * 64 + zz * 16, 16), :] = own
        elif ph == 7:
            for s in range(3):
                cols = pl.ds(pl.multiple_of(512 * s + c * 128, 128), 128)
                ow[:, cols] = gb[c, 512 * s : 512 * s + 512, :].astype(F32) * FACTOR
            rows = pl.ds(pl.multiple_of(c * 128, 128), 128)
            for n in range(4):
                part = gb[c, 1536 + 128 * n : 1664 + 128 * n, :]
                op[rows, 128 * n : 128 * n + 128] = part.astype(F32) * FACTOR

    def advance(c, k):
        receive(c, k - 1)
        if k < 8:
            send(c, k)

    low = lax.broadcasted_iota(jnp.int32, (NT, 128), 1) < 64

    def attend(p, w):
        rows = slice(w * NT, w * NT + NT)

        def cols(s):
            return pl.ds(pl.multiple_of(p * 384 + 128 * s, 128), 128)

        q = qkv[rows, cols(0)] * 0.125
        k = qkv[rows, cols(1)]
        v = qkv[rows, cols(2)]
        ga = gatt[rows, pl.ds(pl.multiple_of(p * 128, 128), 128)]
        kt = k.T
        vt = v.T
        zero = jnp.zeros((), BF16)
        att, dv, dk, dq = [], [], [], []
        for half in range(2):
            here = low if half == 0 else ~low
            kh = jnp.where(here, k, zero)
            vh = jnp.where(here, v, zero)
            lanes = slice(64 * half, 64 * half + 64)
            h = 2 * p + half
            s = dot_nt(kh, q) + bias_t[h][:, 0:NT]
            if w > 0:
                s = s + masks[w - 1][:, 0:NT]
            e = jnp.exp(s - jnp.max(s, 0, keepdims=True))
            prob = e * (1.0 / jnp.sum(e, 0, keepdims=True))
            pb = prob.astype(BF16)
            att.append(dot(vt[lanes], pb))
            dp = dot_nt(vh, ga)
            ds = prob * (dp - jnp.sum(prob * dp, 0, keepdims=True))
            if w == 0:
                dsum[h, :, 0:NT] = ds
            else:
                dsum[h, :, 0:NT] += ds
            db = ds.astype(BF16)
            dv.append(dot(pb, ga))
            dk.append(dot(db, q))
            dq.append(dot(kt[lanes], db) * 0.125)
        dqkv[rows, cols(0)] = jnp.concatenate(dq, 0).T.astype(BF16)
        dqkv[rows, cols(1)] = jnp.where(low, dk[0], dk[1]).astype(BF16)
        dqkv[rows, cols(2)] = jnp.where(low, dv[0], dv[1]).astype(BF16)
        part = dot(jnp.concatenate(att, 0).astype(BF16), gwin[rows, :])
        if w == 0:
            dproj[...] = part
        else:
            dproj[...] += part

    dsum[...] = jnp.zeros((HEADS, NT, 256), F32)

    def pair(p, _):
        for w in range(WINS):
            attend(p, w)
            if w == WINS - 1:
                grads = dot(normt[...], dqkv[:, pl.ds(pl.multiple_of(p * 384, 128), 384)])
                for s in range(3):
                    cb[p, 512 * s : 512 * s + 512, :] = grads[:, 128 * s : 128 * s + 128].astype(BF16)
                for n in range(4):
                    cb[p, 1536 + 128 * n : 1664 + 128 * n, :] = dproj[:, 128 * n : 128 * n + 128].astype(BF16)
                send(p, 0)

            @pl.when(p >= 1)
            def _():
                advance(p - 1, w + 1)

            @pl.when(p >= 2)
            def _():
                advance(p - 2, w + 5)

        return 0

    lax.fori_loop(0, PAIRS, pair, 0)

    def back(n, _):
        rows = pl.ds(pl.multiple_of(n * 256, 256), 256)
        dn[:, rows] = dot_nt(dqkv[...], wp[rows, :])
        return 0

    lax.fori_loop(0, 2, back, 0)
    advance(3, 1)
    advance(2, 5)

    def layer_norm_back(w, sums):
        rows = pl.ds(pl.multiple_of(w * NT, NT), NT)
        hat = x32[rows, :]
        d = dn[rows, :]
        dg = sums[0] + jnp.sum(d * hat, 0, keepdims=True)
        db = sums[1] + jnp.sum(d, 0, keepdims=True)
        g = d * gain
        m1 = jnp.mean(g, -1, keepdims=True)
        m2 = jnp.mean(g * hat, -1, keepdims=True)
        dn[rows, :] = inv[rows, :] * (g - m1 - hat * m2)
        return dg, db

    none = jnp.zeros((1, D), F32)
    dg, db = lax.fori_loop(0, WINS, layer_norm_back, (none, none))

    for name in PIECES:
        start = PIECES[name][0]
        for at, count, src in PLACES[name]:
            s32[start + at : start + at + count, :] = dn[src : src + count, :]
    sndr[...] = s32[...].astype(BF16)

    def homeward(k, name):
        start, _, rows, dlat, dlon = PIECES[name]
        return pltpu.make_async_remote_copy(
            src_ref=sndr.at[pl.ds(start, rows)],
            dst_ref=rcvr.at[pl.ds(start, rows)],
            send_sem=ret_s.at[k],
            recv_sem=ret_r.at[k],
            device_id=beside(-dlat, -dlon),
            device_id_type=MESH,
        )

    rets = [homeward(k, name) for k, name in enumerate("ADBEC")]
    for copy in rets:
        copy.start()

    advance(3, 2)
    advance(2, 6)

    for h in range(HEADS):
        for n in range(2):
            bj.at[n][pl.ds(h, NT, stride=8), :] = dsum[h, :, 128 * n : 128 * n + 128]
    sh[...] = dot(jnp.concatenate([bj[0], bj[1]], 1), picks((256, 384), 1), lax.Precision.HIGHEST)
    tbl[...] = jnp.zeros((HEADS, 768), F32)
    total = jnp.zeros((HEADS, 768), F32)
    rest = jnp.zeros((HEADS, 384), F32)
    for j in range(NT):
        at = place_of(j)
        wide = jnp.concatenate([sh[8 * j : 8 * j + 8, :], rest], 1)
        total = total + (wide if at == 0 else pltpu.roll(wide, at, 1))
    for n in range(6):
        exb[8 * n : 8 * n + 8, :] = total[:, 128 * n : 128 * n + 128]
    for n in range(4):
        exb[48 + n : 49 + n, :] = dg[:, 128 * n : 128 * n + 128]
        exb[52 + n : 53 + n, :] = db[:, 128 * n : 128 * n + 128]
    exb[56:64, :] = jnp.zeros((8, 128), F32)

    def small(k, src, dst, device):
        return pltpu.make_async_remote_copy(
            src_ref=src, dst_ref=dst, send_sem=exs.at[k], recv_sem=exr.at[k],
            device_id=device, device_id_type=MESH,
        )

    def small_ring(axis, at, buf, k, arriving):
        src = buf.at[at]
        out = []
        for d in (1, 2, 3):
            dst = buf.at[(at - d + 4) % 4 if arriving else at]
            out.append(small(k + d - 1, src, dst, peer(axis, d)))
        return out

    def small_step(axis, at, buf, k):
        for copy in small_ring(axis, at, buf, k, True):
            copy.wait_recv()
        return (buf[0] + buf[1]) + (buf[2] + buf[3])

    first = small(0, exb, exc, other)
    first.start()

    advance(3, 3)
    advance(2, 7)

    first.wait_recv()
    exx[xx] = exb[...] + exc[...]
    for copy in small_ring("x", xx, exx, 1, False):
        copy.start()

    advance(3, 4)
    advance(2, 8)

    exy[yy] = small_step("x", xx, exx, 1)
    for copy in small_ring("y", yy, exy, 4, False):
        copy.start()

    advance(3, 5)

    for copy in rets:
        copy.wait_recv()
    s32[...] = rcvr[...].astype(F32)
    for level in (1, 2, 3, 0):
        for row in range(12):
            halves = []
            for half in range(2):
                own, at = half_slab(level, row, half)
                buf = dn if own else s32
                halves.append(buf[at : at + 6, :].astype(BF16).astype(F32))
            both = jnp.concatenate(halves, 0)
            tok[level, row] = (grd[level, row].astype(F32) + both).astype(BF16)
    outs = [pltpu.make_async_copy(tok, out_tok, out_sem.at[0])]
    outs[0].start()

    exz[zz] = small_step("y", yy, exy, 4)
    for copy in small_ring("z", zz, exz, 7, False):
        copy.start()

    advance(3, 6)
    end = small_step("z", zz, exz, 7) * FACTOR
    for n in range(5):
        out_table[:, 128 * n : 128 * n + 128] = end[8 * n : 8 * n + 8]
    out_table[:, 640:RELS] = end[40:48, 0 : RELS - 640]
    for n in range(4):
        out_gain[:, 128 * n : 128 * n + 128] = end[48 + n : 49 + n]
        out_beta[:, 128 * n : 128 * n + 128] = end[52 + n : 53 + n]
    advance(3, 7)
    advance(3, 8)

    outs += [
        pltpu.make_async_copy(ow, out_wqkv, out_sem.at[1]),
        pltpu.make_async_copy(op, out_wproj, out_sem.at[2]),
    ]
    for copy in outs[1:]:
        copy.start()

    for copy in xs + gs + rets + [first]:
        copy.wait_send()
    for axis, at, buf, k in (("x", xx, exx, 1), ("y", yy, exy, 4), ("z", zz, exz, 7)):
        for copy in small_ring(axis, at, buf, k, False):
            copy.wait_send()

    def sent(c, _):
        for ph in range(8):
            for copy in phase_copies(c, ph, False):
                copy.wait_send()
        return 0

    lax.fori_loop(0, PAIRS, sent, 0)
    for copy in outs:
        copy.wait()


def shards(tokens, grad_output, norm_gain, norm_bias, w_qkv, w_proj, rel_bias):
    any_space = pl.BlockSpec(memory_space=pl.ANY)
    vmem = pl.BlockSpec(memory_space=pltpu.VMEM)
    dma = pltpu.SemaphoreType.DMA
    scratch = [
        pltpu.VMEM((4, 12, 12, D), BF16),
        pltpu.VMEM((4, 12, 12, D), BF16),
        pltpu.VMEM((D, 3 * D), BF16),
        pltpu.VMEM((D, D), BF16),
        pltpu.VMEM((TOK, D), F32),
        pltpu.VMEM((TOK, D), F32),
        pltpu.VMEM((SEND_ROWS, D), F32),
        pltpu.VMEM((TOK, 1), F32),
    ]
    scratch += [pltpu.VMEM((SEND_ROWS, D), BF16)] * 6
    scratch += [
        pltpu.VMEM((TOK, D), BF16),
        pltpu.VMEM((D, TOK), BF16),
        pltpu.VMEM((TOK, 3 * D), BF16),
        pltpu.VMEM((TOK, D), BF16),
        pltpu.VMEM((TOK, D), BF16),
        pltpu.VMEM((TOK, 3 * D), BF16),
        pltpu.VMEM((TOK, D), F32),
        pltpu.VMEM((HEADS, 768), F32),
        pltpu.VMEM((HEADS * NT, 384), F32),
        pltpu.VMEM((2, HEADS * NT, 128), F32),
        pltpu.VMEM((HEADS, NT, 256), F32),
        pltpu.VMEM((3, NT, 256), F32),
        pltpu.VMEM((HEADS, NT, 256), F32),
        pltpu.VMEM((128, D), F32),
        pltpu.VMEM((PAIRS, 2048, 128), BF16),
        pltpu.VMEM((PAIRS, 1024, 128), BF16),
        pltpu.VMEM((PAIRS, 1024, 128), BF16),
        pltpu.VMEM((PAIRS, 3, 256, 128), BF16),
        pltpu.VMEM((PAIRS, 256, 128), BF16),
        pltpu.VMEM((PAIRS, 3, 64, 128), BF16),
        pltpu.VMEM((PAIRS, 64, 128), BF16),
        pltpu.VMEM((PAIRS, 3, 16, 128), BF16),
        pltpu.VMEM((PAIRS, 2048, 128), BF16),
        pltpu.VMEM((D, 3 * D), F32),
        pltpu.VMEM((D, D), F32),
        pltpu.VMEM((64, 128), F32),
        pltpu.VMEM((64, 128), F32),
        pltpu.VMEM((4, 64, 128), F32),
        pltpu.VMEM((4, 64, 128), F32),
        pltpu.VMEM((4, 64, 128), F32),
        dma((15,)),
        dma((10,)),
        dma((10,)),
        dma((5,)),
        dma((5,)),
        dma((PAIRS, 20)),
        dma((PAIRS, 20)),
        dma((10,)),
        dma((10,)),
        dma((3,)),
    ]
    out = pl.pallas_call(
        kernel,
        out_shape=(
            jax.ShapeDtypeStruct(tokens.shape, BF16),
            jax.ShapeDtypeStruct((D, 3 * D), F32),
            jax.ShapeDtypeStruct((D, D), F32),
            jax.ShapeDtypeStruct((1, D), F32),
            jax.ShapeDtypeStruct((1, D), F32),
            jax.ShapeDtypeStruct((HEADS, RELS), F32),
        ),
        in_specs=[any_space, any_space, vmem, vmem, any_space, any_space, vmem],
        out_specs=(any_space, any_space, any_space, vmem, vmem, vmem),
        scratch_shapes=scratch,
        compiler_params=pltpu.CompilerParams(
            collective_id=0, has_side_effects=True, vmem_limit_bytes=56 * 1024 * 1024
        ),
    )(tokens, grad_output, norm_gain[None], norm_bias[None], w_qkv, w_proj, rel_bias)
    return out[0], out[1], out[2], out[3][0], out[4][0], out[5]


def solution(mesh):
    grid = P(None, "lat", "lon", None)
    return jax.shard_map(
        shards,
        mesh=mesh,
        in_specs=(grid, grid, P(), P(), P(), P(), P()),
        out_specs=(grid, P(), P(), P(), P(), P()),
        check_vma=False,
    )
```

```python
import functools

import jax
import jax.numpy as jnp
from jax import lax
from jax.experimental import pallas as pl
from jax.experimental.pallas import tpu as pltpu
from jax.sharding import PartitionSpec as P

F32 = jnp.float32
BF16 = jnp.bfloat16
MESH = pl.DeviceIdType.MESH

NT = 144
WINS = 4
TOK = WINS * NT
D = 512
HEADS = 8
PAIRS = 4
RELS = 759
EPS = 1e-5
MASKED = -1e9
FACTOR = 73728 ** (-0.5)

PIECES = (
    ((3, 6), (0, 6), (0, 1, 0, 6), 0, -1),
    ((9, 3), (6, 6), (1, 0, 0, 3), 0, 1),
    ((0, 3), (6, 6), (1, 0, 3, 3), -1, 1),
    ((0, 3), (0, 6), (1, 1, 3, 3), -1, 0),
)
KEPT = (
    ((3, 6), (6, 6), (0, 0, 0, 6)),
    ((9, 3), (0, 6), (1, 1, 0, 3)),
)
LEVELS = ((1, 2), (3, 0))


def place_of(i):
    o6 = i % 6
    a = i // 6 % 6
    oh = i // 36 % 2
    lev = i // 72
    return 253 * lev + 23 * a + 6 * oh + o6


STEPS = (
    (0, 4, "axis"),
    (0, 13, "plane"),
    (1, 11, "axis"),
    (2, 15, "axis"),
)


def dot(a, b, precision=None):
    return lax.dot_general(
        a, b, (((1,), (0,)), ((), ())), precision=precision, preferred_element_type=F32
    )


def dot_nt(a, b):
    return lax.dot_general(a, b, (((1,), (1,)), ((), ())), preferred_element_type=F32)


def kernel(
    tok_hbm, grd_hbm, gain_ref, bias_ref, wqkv_hbm, wproj_hbm, rel_ref,
    out_tok, out_sum, out_small,
    xw, gw, gnat, yw, ret, wp, wproj, x32, t32, inv,
    normed, normt, qkv, gatt, gwin, dqkv, dn,
    tbl, sh, bj, bias_t, masks, dsum, probs, atts,
    cb, rc0, b1, ra, r1, rs, gb,
    exb, exc, exx, exy, exz,
    load_sem, halo_s, halo_r, ret_s, ret_r, core_s, core_r, ax_s, ax_r, rs_s, rs_r, ag_s, ag_r, exs, exr, out_sem,
):
    lon = lax.axis_index("lon")
    lat = lax.axis_index("lat")
    core = lax.rem(lat, 2)
    zz = lax.div(lon, 16) * 2 + lax.div(lat, 2)
    flat = lax.rem(lon, 16)
    yy = lax.div(flat, 4)
    xx = lax.rem(flat, 4)
    me = zz * 16 + flat
    layer_lon = [lax.div(lax.rem(zz + d, 4), 2) * 16 for d in range(4)]
    layer_lat = [lax.rem(lax.rem(zz + d, 4), 2) * 2 + core for d in range(4)]

    def turned(at, d, count):
        return lax.rem(at + d, count)

    def beside(dlat, dlon):
        return (turned(lon, dlon + 32, 32), turned(lat, dlat + 4, 4))

    def peer(axis, d):
        if axis == "x":
            return (lon - xx + turned(xx, d, 4), lat)
        if axis == "y":
            return (lon - yy * 4 + turned(yy, d, 4) * 4, lat)
        return (layer_lon[d] + flat, layer_lat[d])

    other = (lon, lat + 1 - 2 * core)

    def all_chips(act):
        for dz in range(4):

            def one(d, _):
                r = turned(flat, d, 16)
                act((layer_lon[dz] + r, layer_lat[dz]), turned(zz, dz, 4) * 16 + r)
                return 0

            lax.fori_loop(1 if dz == 0 else 0, 16, one, 0)

    barrier = pltpu.get_barrier_semaphore()

    def greet(device):
        pl.semaphore_signal(barrier, inc=1, device_id=device, device_id_type=MESH)

    around = [beside(0, -1), beside(0, 1), beside(-1, 1), beside(1, -1), beside(-1, 0), beside(1, 0), other]
    for device in around:
        greet(device)
    all_chips(lambda device, _: greet(device))

    loads = []

    def load(src, dst):
        loads.append(pltpu.make_async_copy(src, dst, load_sem.at[len(loads)]))
        loads[-1].start()

    def grid_part(ref, rows, cols):
        return ref.at[pl.ds(*rows), pl.ds(*cols)]

    def window_part(ref, at):
        return ref.at[at[0], at[1], pl.ds(at[2], at[3])]

    for rows, cols, at in KEPT:
        load(grid_part(tok_hbm, rows, cols), window_part(xw, at))
    for p in range(PAIRS):
        for n in range(3):
            load(
                wqkv_hbm.at[:, pl.ds(512 * n + 128 * p, 128)],
                wp.at[:, pl.ds(384 * p + 128 * n, 128)],
            )
    for rows, cols, at in KEPT:
        load(grid_part(grd_hbm, rows, cols), window_part(gw, at))
    load(wproj_hbm, wproj)
    load(grd_hbm, gnat)

    def halo(k, piece, src, dst):
        rows, cols, at, dlat, dlon = piece
        return pltpu.make_async_remote_copy(
            src_ref=grid_part(src, rows, cols),
            dst_ref=window_part(dst, at),
            send_sem=halo_s.at[k],
            recv_sem=halo_r.at[k],
            device_id=beside(dlat, dlon),
            device_id_type=MESH,
        )

    xs = [halo(k, piece, tok_hbm, xw) for k, piece in enumerate(PIECES)]
    gs = [halo(4 + k, piece, grd_hbm, gw) for k, piece in enumerate(PIECES)]
    pl.semaphore_wait(barrier, 63 + len(around))
    for copy in xs:
        copy.start()

    tbl[...] = jnp.zeros((HEADS, 768), F32)
    tbl[:, 0:RELS] = rel_ref[...]
    table = tbl[...]
    for j in range(NT):
        at = place_of(j)
        shifted = table if at == 0 else pltpu.roll(table, 768 - at, 1)
        sh[8 * j : 8 * j + 8, :] = shifted[:, 0:384]

    def picks(shape, dim):
        lane = lax.broadcasted_iota(jnp.int32, shape, 1 - dim)
        place = jnp.where(lane < NT, 379 - place_of(lane), -1)
        return (lax.broadcasted_iota(jnp.int32, shape, dim) == place).astype(F32)

    spread = dot(sh[...], picks((384, 256), 0), lax.Precision.HIGHEST)
    for n in range(2):
        bj[n] = spread[:, 128 * n : 128 * n + 128]
    for h in range(HEADS):
        both = jnp.concatenate([bj.at[n][pl.ds(h, NT, stride=8), :] for n in range(2)], 1)
        bias_t[h // 2, :, NT * (h % 2) : NT * (h % 2) + NT] = both[:, 0:NT]

    ti = lax.broadcasted_iota(jnp.int32, (NT, 2 * NT), 0)
    tj = lax.broadcasted_iota(jnp.int32, (NT, 2 * NT), 1) % NT
    lev_cut = ti // 72 != tj // 72
    lat_cut = ((ti // 18) % 2 != (tj // 18) % 2) & (lat == 3)
    masks[0] = jnp.where(lat_cut, MASKED, 0.0)
    masks[1] = jnp.where(lev_cut, MASKED, 0.0)
    masks[2] = jnp.where(lat_cut | lev_cut, MASKED, 0.0)

    for copy in xs:
        copy.wait_send()
    for copy in gs:
        copy.start()

    def spread_rows(ref):
        for block in range(2):
            for half in range(2):
                part = ref[block, half].astype(F32).reshape(NT, D)
                at = (2 * block + half) * NT
                for n in range(4):
                    t32[n, at : at + NT, :] = part[:, 128 * n : 128 * n + 128]

    def level_rows(w, k):
        return pl.ds(288 * (w % 2) + LEVELS[w // 2][k], 72, stride=4)

    def window_rows(w):
        halves = []
        for k in range(2):
            halves.append(jnp.concatenate([t32.at[n][level_rows(w, k), :] for n in range(4)], 1))
        return jnp.concatenate(halves, 0)

    for copy in loads[0:14]:
        copy.wait()
    for copy in xs:
        copy.wait_recv()
    gain = gain_ref[...]
    beta = bias_ref[...]
    spread_rows(xw)
    for w in range(WINS):
        rows = slice(w * NT, w * NT + NT)
        x = window_rows(w)
        centred = x - jnp.mean(x, -1, keepdims=True)
        variance = jnp.mean(centred * centred, -1, keepdims=True)
        scale = lax.rsqrt(variance + EPS)
        hat = centred * scale
        x32[rows, :] = hat
        inv[rows, :] = scale
        normed[rows, :] = (hat * gain + beta).astype(BF16)
    normt[...] = normed[...].T

    def project(n, _):
        cols = pl.ds(pl.multiple_of(n * 256, 256), 256)
        qkv[:, cols] = dot(normed[...], wp[:, cols]).astype(BF16)
        return 0

    lax.fori_loop(0, 6, project, 0)

    def rows_at(start, rows):
        return pl.ds(pl.multiple_of(start, 16), rows)

    def core_copy(c, k, src, dst):
        return pltpu.make_async_remote_copy(
            src_ref=src, dst_ref=dst, send_sem=core_s.at[c, k], recv_sem=core_r.at[c, k],
            device_id=other, device_id_type=MESH,
        )

    def core_in(c):
        return core_copy(c, 0, cb.at[c, rows_at((1 - core) * 1024, 1024)], rc0.at[c])

    def core_out(c, arriving):
        half = 1 - core if arriving else core
        return core_copy(c, 1, gb.at[c, rows_at(core * 1024, 1024)], gb.at[c, rows_at(half * 1024, 1024)])

    def mine(c):
        return gb.at[c, rows_at(core * 1024 + me * 16, 16)]

    def scatter_copy(c, device, to):
        return pltpu.make_async_remote_copy(
            src_ref=b1.at[c, to], dst_ref=rs.at[c, me], send_sem=rs_s.at[c], recv_sem=rs_r.at[c],
            device_id=device, device_id_type=MESH,
        )

    def gather_copy(c, device):
        return pltpu.make_async_remote_copy(
            src_ref=mine(c), dst_ref=mine(c), send_sem=ag_s.at[c], recv_sem=ag_r.at[c],
            device_id=device, device_id_type=MESH,
        )

    def all_of(ref, send_sem, recv_sem):
        return pltpu.make_async_remote_copy(
            src_ref=ref, dst_ref=ref, send_sem=send_sem, recv_sem=recv_sem, device_id=other, device_id_type=MESH
        )

    def all_scattered(c):
        return all_of(rs.at[c, pl.ds(0, 63)], rs_s.at[c], rs_r.at[c])

    def all_gathered(c):
        return all_of(gb.at[c, pl.ds(0, 1008)], ag_s.at[c], ag_r.at[c])

    def chunk_done(c):
        core_in(c).start()

    def scatter(c):
        core_in(c).wait_recv()
        own = cb[c, rows_at(core * 1024, 1024), :].astype(F32)
        b1[c] = (own + rc0[c].astype(F32)).astype(BF16).reshape(64, 16, 128)
        rs[c, me] = b1[c, me]
        all_chips(lambda device, to: scatter_copy(c, device, to).start())

    def gather(c):
        all_scattered(c).wait_recv()
        total = jnp.sum(rs[c].astype(F32), 0)
        gb[c, rows_at(core * 1024 + me * 16, 16), :] = total.astype(BF16)
        all_chips(lambda device, _: gather_copy(c, device).start())

    def share(c):
        all_gathered(c).wait_recv()
        core_out(c, False).start()

    def place_in(c):
        return ((xx, zz * 4 + yy), (yy, xx * 4 + zz), (zz, yy * 4 + xx))[c]

    def plane_chips(c, act):
        for d in range(1, 16):
            i, j = divmod(d, 4)
            if c == 0:
                y = turned(yy, j, 4)
                act((layer_lon[i] + y * 4 + xx, layer_lat[i]), turned(zz, i, 4) * 4 + y)
            elif c == 1:
                x = turned(xx, i, 4)
                act((layer_lon[j] + yy * 4 + x, layer_lat[j]), x * 4 + turned(zz, j, 4))
            else:
                r = turned(yy, i, 4) * 4 + turned(xx, j, 4)
                act((lon - flat + r, lat), r)

    def axis_copies(c, back, arriving):
        a, q = place_in(c)
        out = []
        for d in (1, 2, 3):
            to = turned(a, d, 4)
            if back:
                at = turned(a, 4 - d, 4) if arriving else a
                src = gb.at[c, rows_at(core * 1024 + a * 256, 256)]
                dst = gb.at[c, rows_at(core * 1024 + at * 256, 256)]
            else:
                src = b1.at[c, pl.ds(to * 16, 16)]
                dst = ra.at[c, d - 1]
            k = 3 * back + d - 1
            out.append(
                pltpu.make_async_remote_copy(
                    src_ref=src, dst_ref=dst, send_sem=ax_s.at[c, k], recv_sem=ax_r.at[c, k],
                    device_id=peer("xyz"[c], d), device_id_type=MESH,
                )
            )
        return out

    def piece(c):
        a, q = place_in(c)
        return rows_at(core * 1024 + a * 256 + q * 16, 16)

    def to_plane(c, back):
        _, q = place_in(c)

        def one(device, to):
            if back:
                src = dst = gb.at[c, piece(c)]
            else:
                src, dst = r1.at[c, to], rs.at[c, q]
            pltpu.make_async_remote_copy(
                src_ref=src, dst_ref=dst,
                send_sem=(ag_s if back else rs_s).at[c], recv_sem=(ag_r if back else rs_r).at[c],
                device_id=device, device_id_type=MESH,
            ).start()

        plane_chips(c, one)

    def plane_scattered(c):
        return all_of(rs.at[c, pl.ds(0, 15)], rs_s.at[c], rs_r.at[c])

    def plane_gathered(c):
        return all_of(gb.at[c, pl.ds(0, 240)], ag_s.at[c], ag_r.at[c])

    def scatter_axis(c):
        core_in(c).wait_recv()
        own = cb[c, rows_at(core * 1024, 1024), :].astype(F32)
        b1[c] = (own + rc0[c].astype(F32)).astype(BF16).reshape(64, 16, 128)
        for copy in axis_copies(c, False, False):
            copy.start()

    def scatter_plane(c):
        a, q = place_in(c)
        for copy in axis_copies(c, False, True):
            copy.wait_recv()
        own = b1[c, pl.ds(a * 16, 16)].astype(F32)
        for d in range(3):
            own = own + ra[c, d].astype(F32)
        r1[c] = own.astype(BF16)
        rs[c, q] = r1[c, q]
        to_plane(c, False)

    def gather_plane(c):
        plane_scattered(c).wait_recv()
        gb[c, piece(c), :] = jnp.sum(rs[c, 0:16].astype(F32), 0).astype(BF16)
        to_plane(c, True)

    def gather_axis(c):
        plane_gathered(c).wait_recv()
        for copy in axis_copies(c, True, False):
            copy.start()

    def share_axis(c):
        for copy in axis_copies(c, True, True):
            copy.wait_recv()
        core_out(c, False).start()

    def out_copy(c):
        return pltpu.make_async_copy(gb.at[c], out_sum.at[c], out_sem.at[1 + c])

    def finish(c):
        core_out(c, True).wait_recv()
        out_copy(c).start()

    low = lax.broadcasted_iota(jnp.int32, (NT, 128), 1) < 64
    zero = jnp.zeros((), BF16)

    def by_head(x):
        return jnp.concatenate([jnp.where(low, x, zero), jnp.where(low, zero, x)], 0)

    def part_of(p, s):
        return pl.ds(pl.multiple_of(p * 384 + 128 * s, 128), 128)

    def forward(p, w):
        rows = slice(w * NT, w * NT + NT)
        s = dot_nt(qkv[rows, part_of(p, 1)], by_head(qkv[rows, part_of(p, 0)] * 0.125)) + bias_t[p]
        if w > 0:
            s = s + masks[w - 1]
        e = jnp.exp(s - jnp.max(s, 0, keepdims=True))
        prob = e * (1.0 / jnp.sum(e, 0, keepdims=True))
        probs[p, w] = prob
        both = dot(qkv[rows, part_of(p, 2)].T, prob.astype(BF16))
        att = jnp.concatenate([both[0:64, 0:NT], both[64:128, NT : 2 * NT]], 0)
        atts[w, pl.ds(pl.multiple_of(p * 128, 128), 128), :] = att.astype(BF16)

    def backward(p, w):
        rows = slice(w * NT, w * NT + NT)
        q2 = by_head(qkv[rows, part_of(p, 0)] * 0.125)
        ga2 = by_head(gatt[rows, pl.ds(pl.multiple_of(p * 128, 128), 128)])
        prob = probs[p, w]
        dp = dot_nt(qkv[rows, part_of(p, 2)], ga2)
        ds = prob * (dp - jnp.sum(prob * dp, 0, keepdims=True))
        if w == 0:
            dsum[p] = ds
        else:
            dsum[p] += ds
        db = ds.astype(BF16)
        dq = (dot(qkv[rows, part_of(p, 1)].T, db) * 0.125).astype(BF16).T
        dqkv[rows, part_of(p, 0)] = jnp.where(low, dq[0:NT], dq[NT : 2 * NT])
        dqkv[rows, part_of(p, 1)] = dot(db, q2).astype(BF16)
        dqkv[rows, part_of(p, 2)] = dot(prob.astype(BF16), ga2).astype(BF16)

    def forward_pair(p, _):
        for w in range(WINS):
            forward(p, w)
        return 0

    lax.fori_loop(0, PAIRS, forward_pair, 0)

    for copy in loads[14:]:
        copy.wait()
    for copy in gs:
        copy.wait_recv()
    spread_rows(gw)
    for w in range(WINS):
        gwin[w * NT : w * NT + NT, :] = window_rows(w).astype(BF16)

    def project_g(n, _):
        cols = pl.ds(pl.multiple_of(n * 256, 256), 256)
        gatt[:, cols] = dot_nt(gwin[...], wproj[cols, :]).astype(BF16)
        return 0

    lax.fori_loop(0, 2, project_g, 0)

    dproj = dot(atts[0], gwin[0:NT, :])
    for w in range(1, WINS):
        dproj = dproj + dot(atts[w], gwin[w * NT : w * NT + NT, :])
    for n in range(4):
        cb[0, 512 * n : 512 * n + 512, :] = dproj[:, 128 * n : 128 * n + 128].astype(BF16)
    chunk_done(0)

    def pair(p, _):
        for w in range(WINS):
            backward(p, w)
            if w == WINS - 1:
                cols = pl.ds(pl.multiple_of(p * 384, 128), 384)
                grads = dot(normt[...], dqkv[:, cols])
                for s in range(3):
                    block = 3 * p + s
                    cb[1 + block // 4, rows_at(block % 4 * 512, 512), :] = grads[:, 128 * s : 128 * s + 128].astype(BF16)

                @pl.when(p >= 1)
                def _():
                    chunk_done(p)

                part = dot_nt(dqkv[:, cols], wp[:, cols])

                @pl.when(p == 0)
                def _():
                    dn[...] = part

                @pl.when(p > 0)
                def _():
                    dn[...] += part

            for c, at, step in STEPS:
                if at % 4 == w:
                    call = {"axis": scatter_axis, "plane": scatter_plane}[step]
                    pl.when(p == at // 4)(functools.partial(call, c))
        return 0

    lax.fori_loop(0, PAIRS, pair, 0)

    for h in range(HEADS):
        one = dsum[h // 2, :, NT * (h % 2) : NT * (h % 2) + NT]
        one = jnp.concatenate([one, jnp.zeros((NT, 256 - NT), F32)], 1)
        for n in range(2):
            bj.at[n][pl.ds(h, NT, stride=8), :] = one[:, 128 * n : 128 * n + 128]
    sh[...] = dot(jnp.concatenate([bj[0], bj[1]], 1), picks((256, 384), 1), lax.Precision.HIGHEST)
    total = jnp.zeros((HEADS, 768), F32)
    rest = jnp.zeros((HEADS, 384), F32)
    for j in range(NT):
        at = place_of(j)
        wide = jnp.concatenate([sh[8 * j : 8 * j + 8, :], rest], 1)
        total = total + (wide if at == 0 else pltpu.roll(wide, at, 1))
    for n in range(6):
        exb[8 * n : 8 * n + 8, :] = total[:, 128 * n : 128 * n + 128]
    dg = jnp.zeros((1, D), F32)
    db = jnp.zeros((1, D), F32)
    for w in range(WINS):
        rows = slice(w * NT, w * NT + NT)
        d = dn[rows, :]
        dg = dg + jnp.sum(d * x32[rows, :], 0, keepdims=True)
        db = db + jnp.sum(d, 0, keepdims=True)
    for n in range(4):
        exb[48 + n : 49 + n, :] = dg[:, 128 * n : 128 * n + 128]
        exb[52 + n : 53 + n, :] = db[:, 128 * n : 128 * n + 128]
    exb[56:64, :] = jnp.zeros((8, 128), F32)

    def small(k, src, dst, device):
        return pltpu.make_async_remote_copy(
            src_ref=src, dst_ref=dst, send_sem=exs.at[k], recv_sem=exr.at[k],
            device_id=device, device_id_type=MESH,
        )

    def small_ring(axis, at, buf, k, arriving):
        src = buf.at[at]
        out = []
        for d in (1, 2, 3):
            dst = buf.at[turned(at, 4 - d, 4) if arriving else at]
            out.append(small(k + d - 1, src, dst, peer(axis, d)))
        return out

    def small_step(axis, at, buf, k):
        for copy in small_ring(axis, at, buf, k, True):
            copy.wait_recv()
        return (buf[0] + buf[1]) + (buf[2] + buf[3])

    first = small(0, exb, exc, other)
    first.start()
    scatter(3)
    gather_plane(0)
    scatter_plane(1)

    for w in range(WINS):
        rows = slice(w * NT, w * NT + NT)
        hat = x32[rows, :]
        g = dn[rows, :] * gain
        m1 = jnp.mean(g, -1, keepdims=True)
        m2 = jnp.mean(g * hat, -1, keepdims=True)
        branch = inv[rows, :] * (g - m1 - hat * m2)
        for k in range(2):
            for n in range(4):
                t32.at[n][level_rows(w, k), :] = branch[72 * k : 72 * k + 72, 128 * n : 128 * n + 128]
    for block in range(2):
        for half in range(2):
            at = (2 * block + half) * NT
            part = jnp.concatenate([t32[n, at : at + NT, :] for n in range(4)], 1)
            yw[block, half] = part.reshape(6, 6, 4, D).astype(BF16)

    def homeward(k, piece):
        rows, cols, at, dlat, dlon = piece
        return pltpu.make_async_remote_copy(
            src_ref=window_part(yw, at),
            dst_ref=grid_part(ret, rows, cols),
            send_sem=ret_s.at[k],
            recv_sem=ret_r.at[k],
            device_id=beside(-dlat, -dlon),
            device_id_type=MESH,
        )

    rets = [homeward(k, piece) for k, piece in enumerate(PIECES)]
    for copy in rets:
        copy.start()
    kept = []
    for k, (rows, cols, at) in enumerate(KEPT):
        kept.append(pltpu.make_async_copy(window_part(yw, at), grid_part(ret, rows, cols), load_sem.at[k]))
        kept[-1].start()

    scatter_plane(2)
    first.wait_recv()
    exx[xx] = exb[...] + exc[...]
    for copy in small_ring("x", xx, exx, 1, False):
        copy.start()
    gather_plane(1)
    gather_axis(0)
    gather_plane(2)
    exy[yy] = small_step("x", xx, exx, 1)
    for copy in small_ring("y", yy, exy, 4, False):
        copy.start()
    gather(3)

    for copy in kept:
        copy.wait()
    for copy in rets:
        copy.wait_recv()
    gnat[...] = (gnat[...].astype(F32) + ret[...].astype(F32)).astype(BF16)
    token_copy = pltpu.make_async_copy(gnat, out_tok, out_sem.at[0])
    token_copy.start()

    share_axis(0)
    gather_axis(1)
    gather_axis(2)
    exz[zz] = small_step("y", yy, exy, 4)
    for copy in small_ring("z", zz, exz, 7, False):
        copy.start()
    finish(0)
    share(3)
    share_axis(1)
    share_axis(2)
    finish(3)
    out_small[...] = small_step("z", zz, exz, 7) * FACTOR
    finish(1)
    finish(2)

    for copy in gs + rets + [first]:
        copy.wait_send()
    for axis, at, buf, k in (("x", xx, exx, 1), ("y", yy, exy, 4), ("z", zz, exz, 7)):
        for copy in small_ring(axis, at, buf, k, False):
            copy.wait_send()
    for c in range(PAIRS):
        core_in(c).wait_send()
        if c == 3:
            all_scattered(c).wait_send()
            all_gathered(c).wait_send()
        else:
            plane_scattered(c).wait_send()
            plane_gathered(c).wait_send()
            for copy in axis_copies(c, False, False) + axis_copies(c, True, False):
                copy.wait_send()
        core_out(c, False).wait_send()
        out_copy(c).wait()
    token_copy.wait()


def finish_kernel(tok_in, sum_hbm, small, out_tok, out_wqkv, out_wproj, out_gain, out_beta, out_table, gb, ow, op, tok, sems):
    tokens_in = pltpu.make_async_copy(tok_in, tok, sems.at[0])
    tokens = pltpu.make_async_copy(tok, out_tok, sems.at[21])
    loads = [pltpu.make_async_copy(sum_hbm.at[c], gb.at[c], sems.at[1 + c]) for c in range(PAIRS)]
    for copy in loads:
        copy.start()
    tokens_in.start()
    outs = []
    for c in range(PAIRS):
        loads[c].wait()
        for n in range(4):
            part = gb[c, 512 * n : 512 * n + 512, :].astype(F32) * FACTOR
            if c == 0:
                op[:, 128 * n : 128 * n + 128] = part
            else:
                pair, kind = divmod(4 * (c - 1) + n, 3)
                cols = slice(512 * kind + 128 * pair, 512 * kind + 128 * pair + 128)
                ow[:, cols] = part
                outs.append(pltpu.make_async_copy(ow.at[:, cols], out_wqkv.at[:, cols], sems.at[5 + 4 * c + n]))
                outs[-1].start()
        if c == 0:
            outs.append(pltpu.make_async_copy(op, out_wproj, sems.at[5]))
            outs[-1].start()
    for n in range(5):
        out_table[:, 128 * n : 128 * n + 128] = small[8 * n : 8 * n + 8, :]
    out_table[:, 640:RELS] = small[40:48, 0 : RELS - 640]
    for n in range(4):
        out_gain[:, 128 * n : 128 * n + 128] = small[48 + n : 49 + n, :]
        out_beta[:, 128 * n : 128 * n + 128] = small[52 + n : 53 + n, :]
    tokens_in.wait()
    tokens.start()
    for copy in outs + [tokens]:
        copy.wait()


def shards(tokens, grad_output, norm_gain, norm_bias, w_qkv, w_proj, rel_bias):
    any_space = pl.BlockSpec(memory_space=pl.ANY)
    vmem = pl.BlockSpec(memory_space=pltpu.VMEM)
    dma = pltpu.SemaphoreType.DMA
    by_window = (2, 2, 6, 6, 4, D)
    by_grid = (12, 12, 4, D)
    scratch = [
        pltpu.VMEM(by_window, BF16),
        pltpu.VMEM(by_window, BF16),
        pltpu.VMEM(by_grid, BF16),
        pltpu.VMEM(by_window, BF16),
        pltpu.VMEM(by_grid, BF16),
        pltpu.VMEM((D, 3 * D), BF16),
        pltpu.VMEM((D, D), BF16),
        pltpu.VMEM((TOK, D), F32),
        pltpu.VMEM((4, TOK, 128), F32),
        pltpu.VMEM((TOK, 1), F32),
        pltpu.VMEM((TOK, D), BF16),
        pltpu.VMEM((D, TOK), BF16),
        pltpu.VMEM((TOK, 3 * D), BF16),
        pltpu.VMEM((TOK, D), BF16),
        pltpu.VMEM((TOK, D), BF16),
        pltpu.VMEM((TOK, 3 * D), BF16),
        pltpu.VMEM((TOK, D), F32),
        pltpu.VMEM((HEADS, 768), F32),
        pltpu.VMEM((HEADS * NT, 384), F32),
        pltpu.VMEM((2, HEADS * NT, 128), F32),
        pltpu.VMEM((PAIRS, NT, 2 * NT), F32),
        pltpu.VMEM((3, NT, 2 * NT), F32),
        pltpu.VMEM((PAIRS, NT, 2 * NT), F32),
        pltpu.VMEM((PAIRS, WINS, NT, 2 * NT), F32),
        pltpu.VMEM((WINS, D, NT), BF16),
        pltpu.VMEM((PAIRS, 2048, 128), BF16),
        pltpu.VMEM((PAIRS, 1024, 128), BF16),
        pltpu.VMEM((PAIRS, 64, 16, 128), BF16),
        pltpu.VMEM((3, 3, 16, 16, 128), BF16),
        pltpu.VMEM((3, 16, 16, 128), BF16),
        pltpu.VMEM((PAIRS, 64, 16, 128), BF16),
        pltpu.VMEM((PAIRS, 2048, 128), BF16),
        pltpu.VMEM((64, 128), F32),
        pltpu.VMEM((64, 128), F32),
        pltpu.VMEM((4, 64, 128), F32),
        pltpu.VMEM((4, 64, 128), F32),
        pltpu.VMEM((4, 64, 128), F32),
        dma((18,)),
        dma((8,)),
        dma((8,)),
        dma((4,)),
        dma((4,)),
        dma((PAIRS, 2)),
        dma((PAIRS, 2)),
        dma((3, 6)),
        dma((3, 6)),
        dma((PAIRS,)),
        dma((PAIRS,)),
        dma((PAIRS,)),
        dma((PAIRS,)),
        dma((10,)),
        dma((10,)),
        dma((5,)),
    ]
    tok_out, summed, small = pl.pallas_call(
        kernel,
        out_shape=(
            jax.ShapeDtypeStruct(by_grid, BF16),
            jax.ShapeDtypeStruct((PAIRS, 2048, 128), BF16),
            jax.ShapeDtypeStruct((64, 128), F32),
        ),
        in_specs=[any_space, any_space, vmem, vmem, any_space, any_space, vmem],
        out_specs=(any_space, any_space, vmem),
        scratch_shapes=scratch,
        compiler_params=pltpu.CompilerParams(
            collective_id=0, has_side_effects=True, vmem_limit_bytes=56 * 1024 * 1024
        ),
    )(
        tokens.transpose(1, 2, 0, 3),
        grad_output.transpose(1, 2, 0, 3),
        norm_gain[None],
        norm_bias[None],
        w_qkv,
        w_proj,
        rel_bias,
    )
    out = pl.pallas_call(
        finish_kernel,
        out_shape=(
            jax.ShapeDtypeStruct(by_grid, BF16),
            jax.ShapeDtypeStruct((D, 3 * D), F32),
            jax.ShapeDtypeStruct((D, D), F32),
            jax.ShapeDtypeStruct((1, D), F32),
            jax.ShapeDtypeStruct((1, D), F32),
            jax.ShapeDtypeStruct((HEADS, RELS), F32),
        ),
        in_specs=[any_space, any_space, vmem],
        out_specs=(any_space, any_space, any_space, vmem, vmem, vmem),
        scratch_shapes=[
            pltpu.VMEM((PAIRS, 2048, 128), BF16),
            pltpu.VMEM((D, 3 * D), F32),
            pltpu.VMEM((D, D), F32),
            pltpu.VMEM(by_grid, BF16),
            dma((22,)),
        ],
        compiler_params=pltpu.CompilerParams(vmem_limit_bytes=60 * 1024 * 1024),
    )(tok_out, summed, small)
    return out[0].transpose(2, 0, 1, 3), out[1], out[2], out[3][0], out[4][0], out[5]


def solution(mesh):
    grid = P(None, "lat", "lon", None)
    return jax.shard_map(
        shards,
        mesh=mesh,
        in_specs=(grid, grid, P(), P(), P(), P(), P()),
        out_specs=(grid, P(), P(), P(), P(), P()),
        check_vma=False,
    )
```

```python
import functools

import jax
import jax.numpy as jnp
from jax import lax
from jax.experimental import pallas as pl
from jax.experimental.pallas import tpu as pltpu
from jax.sharding import PartitionSpec as P

F32 = jnp.float32
BF16 = jnp.bfloat16
MESH = pl.DeviceIdType.MESH

NT = 144
WINS = 4
TOK = WINS * NT
D = 512
HEADS = 8
PAIRS = 4
RELS = 759
EPS = 1e-5
MASKED = -1e9
FACTOR = 73728 ** (-0.5)

PIECES = (
    ((3, 6), (0, 6), (0, 1, 0, 6), 0, -1),
    ((9, 3), (6, 6), (1, 0, 0, 3), 0, 1),
    ((0, 3), (6, 6), (1, 0, 3, 3), -1, 1),
    ((0, 3), (0, 6), (1, 1, 3, 3), -1, 0),
)
KEPT = (
    ((3, 6), (6, 6), (0, 0, 0, 6)),
    ((9, 3), (0, 6), (1, 1, 0, 3)),
)
LEVELS = ((1, 2), (3, 0))


def place_of(i):
    o6 = i % 6
    a = i // 6 % 6
    oh = i // 36 % 2
    lev = i // 72
    return 253 * lev + 23 * a + 6 * oh + o6


STEPS = (
    (0, 4, "axis"),
    (0, 13, "plane"),
    (1, 11, "axis"),
    (2, 15, "axis"),
)


def dot(a, b, precision=None):
    return lax.dot_general(
        a, b, (((1,), (0,)), ((), ())), precision=precision, preferred_element_type=F32
    )


def dot_nt(a, b):
    return lax.dot_general(a, b, (((1,), (1,)), ((), ())), preferred_element_type=F32)


def kernel(
    tok_hbm, grd_hbm, gain_ref, bias_ref, wqkv_hbm, wproj_hbm, rel_ref,
    out_tok, out_sum, out_small,
    xw, gw, gnat, yw, ret, wp, wproj, x32, t32, inv,
    normed, normt, qkv, gatt, gwin, dqkv, dn,
    tbl, sh, bj, bias_t, masks, dsum, probs, atts,
    cb, rc0, b1, ra, r1, rs, gb,
    exb, exc, exx, exy, exz,
    load_sem, halo_s, halo_r, ret_s, ret_r, core_s, core_r, ax_s, ax_r, rs_s, rs_r, ag_s, ag_r, exs, exr, out_sem,
):
    lon = lax.axis_index("lon")
    lat = lax.axis_index("lat")
    core = lax.rem(lat, 2)
    zz = lax.div(lon, 16) * 2 + lax.div(lat, 2)
    flat = lax.rem(lon, 16)
    yy = lax.div(flat, 4)
    xx = lax.rem(flat, 4)
    me = zz * 16 + flat
    layer_lon = [lax.div(lax.rem(zz + d, 4), 2) * 16 for d in range(4)]
    layer_lat = [lax.rem(lax.rem(zz + d, 4), 2) * 2 + core for d in range(4)]

    def turned(at, d, count):
        return lax.rem(at + d, count)

    def beside(dlat, dlon):
        return (turned(lon, dlon + 32, 32), turned(lat, dlat + 4, 4))

    def peer(axis, d):
        if axis == "x":
            return (lon - xx + turned(xx, d, 4), lat)
        if axis == "y":
            return (lon - yy * 4 + turned(yy, d, 4) * 4, lat)
        return (layer_lon[d] + flat, layer_lat[d])

    other = (lon, lat + 1 - 2 * core)

    def all_chips(act):
        for dz in range(4):

            def one(d, _):
                r = turned(flat, d, 16)
                act((layer_lon[dz] + r, layer_lat[dz]), turned(zz, dz, 4) * 16 + r)
                return 0

            lax.fori_loop(1 if dz == 0 else 0, 16, one, 0)

    barrier = pltpu.get_barrier_semaphore()

    def greet(device):
        pl.semaphore_signal(barrier, inc=1, device_id=device, device_id_type=MESH)

    around = [beside(0, -1), beside(0, 1), beside(-1, 1), beside(1, -1), beside(-1, 0), beside(1, 0), other]
    for device in around:
        greet(device)
    all_chips(lambda device, _: greet(device))

    loads = []

    def load(src, dst):
        loads.append(pltpu.make_async_copy(src, dst, load_sem.at[len(loads)]))
        loads[-1].start()

    def grid_part(ref, rows, cols):
        return ref.at[pl.ds(*rows), pl.ds(*cols)]

    def window_part(ref, at):
        return ref.at[at[0], at[1], pl.ds(at[2], at[3])]

    for rows, cols, at in KEPT:
        load(grid_part(tok_hbm, rows, cols), window_part(xw, at))
    for p in range(PAIRS):
        for n in range(3):
            load(
                wqkv_hbm.at[:, pl.ds(512 * n + 128 * p, 128)],
                wp.at[:, pl.ds(384 * p + 128 * n, 128)],
            )
    for rows, cols, at in KEPT:
        load(grid_part(grd_hbm, rows, cols), window_part(gw, at))
    load(wproj_hbm, wproj)
    load(grd_hbm, gnat)

    def halo(k, piece, src, dst):
        rows, cols, at, dlat, dlon = piece
        return pltpu.make_async_remote_copy(
            src_ref=grid_part(src, rows, cols),
            dst_ref=window_part(dst, at),
            send_sem=halo_s.at[k],
            recv_sem=halo_r.at[k],
            device_id=beside(dlat, dlon),
            device_id_type=MESH,
        )

    xs = [halo(k, piece, tok_hbm, xw) for k, piece in enumerate(PIECES)]
    gs = [halo(4 + k, piece, grd_hbm, gw) for k, piece in enumerate(PIECES)]
    pl.semaphore_wait(barrier, 63 + len(around))
    for copy in xs:
        copy.start()

    tbl[...] = jnp.zeros((HEADS, 768), F32)
    tbl[:, 0:RELS] = rel_ref[...]
    table = tbl[...]
    for j in range(NT):
        at = place_of(j)
        shifted = table if at == 0 else pltpu.roll(table, 768 - at, 1)
        sh[8 * j : 8 * j + 8, :] = shifted[:, 0:384]

    def picks(shape, dim):
        lane = lax.broadcasted_iota(jnp.int32, shape, 1 - dim)
        place = jnp.where(lane < NT, 379 - place_of(lane), -1)
        return (lax.broadcasted_iota(jnp.int32, shape, dim) == place).astype(F32)

    spread = dot(sh[...], picks((384, 256), 0), lax.Precision.HIGHEST)
    for n in range(2):
        bj[n] = spread[:, 128 * n : 128 * n + 128]
    for h in range(HEADS):
        both = jnp.concatenate([bj.at[n][pl.ds(h, NT, stride=8), :] for n in range(2)], 1)
        bias_t[h // 2, :, NT * (h % 2) : NT * (h % 2) + NT] = both[:, 0:NT]

    ti = lax.broadcasted_iota(jnp.int32, (NT, 2 * NT), 0)
    tj = lax.broadcasted_iota(jnp.int32, (NT, 2 * NT), 1) % NT
    lev_cut = ti // 72 != tj // 72
    lat_cut = ((ti // 18) % 2 != (tj // 18) % 2) & (lat == 3)
    masks[0] = jnp.where(lat_cut, MASKED, 0.0)
    masks[1] = jnp.where(lev_cut, MASKED, 0.0)
    masks[2] = jnp.where(lat_cut | lev_cut, MASKED, 0.0)

    for copy in xs:
        copy.wait_send()
    for copy in gs:
        copy.start()

    def spread_rows(ref):
        for block in range(2):
            for half in range(2):
                part = ref[block, half].astype(F32).reshape(NT, D)
                at = (2 * block + half) * NT
                for n in range(4):
                    t32[n, at : at + NT, :] = part[:, 128 * n : 128 * n + 128]

    def level_rows(w, k):
        return pl.ds(288 * (w % 2) + LEVELS[w // 2][k], 72, stride=4)

    def window_rows(w):
        halves = []
        for k in range(2):
            halves.append(jnp.concatenate([t32.at[n][level_rows(w, k), :] for n in range(4)], 1))
        return jnp.concatenate(halves, 0)

    for copy in loads[0:14]:
        copy.wait()
    for copy in xs:
        copy.wait_recv()
    gain = gain_ref[...]
    beta = bias_ref[...]
    spread_rows(xw)
    for w in range(WINS):
        rows = slice(w * NT, w * NT + NT)
        x = window_rows(w)
        centred = x - jnp.mean(x, -1, keepdims=True)
        variance = jnp.mean(centred * centred, -1, keepdims=True)
        scale = lax.rsqrt(variance + EPS)
        hat = centred * scale
        x32[rows, :] = hat
        inv[rows, :] = scale
        normed[rows, :] = (hat * gain + beta).astype(BF16)
    normt[...] = normed[...].T

    def project(n, _):
        cols = pl.ds(pl.multiple_of(n * 256, 256), 256)
        qkv[:, cols] = dot(normed[...], wp[:, cols]).astype(BF16)
        return 0

    lax.fori_loop(0, 6, project, 0)

    def rows_at(start, rows):
        return pl.ds(pl.multiple_of(start, 16), rows)

    def core_copy(c, k, src, dst):
        return pltpu.make_async_remote_copy(
            src_ref=src, dst_ref=dst, send_sem=core_s.at[c, k], recv_sem=core_r.at[c, k],
            device_id=other, device_id_type=MESH,
        )

    def core_in(c):
        return core_copy(c, 0, cb.at[c, rows_at((1 - core) * 1024, 1024)], rc0.at[c])

    def core_out(c, arriving):
        half = 1 - core if arriving else core
        return core_copy(c, 1, gb.at[c, rows_at(core * 1024, 1024)], gb.at[c, rows_at(half * 1024, 1024)])

    def mine(c):
        return gb.at[c, rows_at(core * 1024 + me * 16, 16)]

    def scatter_copy(c, device, to):
        return pltpu.make_async_remote_copy(
            src_ref=b1.at[c, to], dst_ref=rs.at[c, me], send_sem=rs_s.at[c], recv_sem=rs_r.at[c],
            device_id=device, device_id_type=MESH,
        )

    def gather_copy(c, device):
        return pltpu.make_async_remote_copy(
            src_ref=mine(c), dst_ref=mine(c), send_sem=ag_s.at[c], recv_sem=ag_r.at[c],
            device_id=device, device_id_type=MESH,
        )

    def all_of(ref, send_sem, recv_sem):
        return pltpu.make_async_remote_copy(
            src_ref=ref, dst_ref=ref, send_sem=send_sem, recv_sem=recv_sem, device_id=other, device_id_type=MESH
        )

    def all_scattered(c):
        return all_of(rs.at[c, pl.ds(0, 63)], rs_s.at[c], rs_r.at[c])

    def all_gathered(c):
        return all_of(gb.at[c, pl.ds(0, 1008)], ag_s.at[c], ag_r.at[c])

    def chunk_done(c):
        core_in(c).start()

    def scatter(c):
        core_in(c).wait_recv()
        own = cb[c, rows_at(core * 1024, 1024), :].astype(F32)
        b1[c] = (own + rc0[c].astype(F32)).astype(BF16).reshape(64, 16, 128)
        rs[c, me] = b1[c, me]
        all_chips(lambda device, to: scatter_copy(c, device, to).start())

    def gather(c):
        all_scattered(c).wait_recv()
        total = jnp.sum(rs[c].astype(F32), 0)
        gb[c, rows_at(core * 1024 + me * 16, 16), :] = total.astype(BF16)
        all_chips(lambda device, _: gather_copy(c, device).start())

    def share(c):
        all_gathered(c).wait_recv()
        core_out(c, False).start()

    def place_in(c):
        return ((xx, zz * 4 + yy), (yy, xx * 4 + zz), (zz, yy * 4 + xx))[c]

    def plane_chips(c, act):
        for d in range(1, 16):
            i, j = divmod(d, 4)
            if c == 0:
                y = turned(yy, j, 4)
                act((layer_lon[i] + y * 4 + xx, layer_lat[i]), turned(zz, i, 4) * 4 + y)
            elif c == 1:
                x = turned(xx, i, 4)
                act((layer_lon[j] + yy * 4 + x, layer_lat[j]), x * 4 + turned(zz, j, 4))
            else:
                r = turned(yy, i, 4) * 4 + turned(xx, j, 4)
                act((lon - flat + r, lat), r)

    def axis_copies(c, back, arriving):
        a, q = place_in(c)
        out = []
        for d in (1, 2, 3):
            to = turned(a, d, 4)
            if back:
                at = turned(a, 4 - d, 4) if arriving else a
                src = gb.at[c, rows_at(core * 1024 + a * 256, 256)]
                dst = gb.at[c, rows_at(core * 1024 + at * 256, 256)]
            else:
                src = b1.at[c, pl.ds(to * 16, 16)]
                dst = ra.at[c, d - 1]
            k = 3 * back + d - 1
            out.append(
                pltpu.make_async_remote_copy(
                    src_ref=src, dst_ref=dst, send_sem=ax_s.at[c, k], recv_sem=ax_r.at[c, k],
                    device_id=peer("xyz"[c], d), device_id_type=MESH,
                )
            )
        return out

    def piece(c):
        a, q = place_in(c)
        return rows_at(core * 1024 + a * 256 + q * 16, 16)

    def to_plane(c, back):
        _, q = place_in(c)

        def one(device, to):
            if back:
                src = dst = gb.at[c, piece(c)]
            else:
                src, dst = r1.at[c, to], rs.at[c, q]
            pltpu.make_async_remote_copy(
                src_ref=src, dst_ref=dst,
                send_sem=(ag_s if back else rs_s).at[c], recv_sem=(ag_r if back else rs_r).at[c],
                device_id=device, device_id_type=MESH,
            ).start()

        plane_chips(c, one)

    def plane_scattered(c):
        return all_of(rs.at[c, pl.ds(0, 15)], rs_s.at[c], rs_r.at[c])

    def plane_gathered(c):
        return all_of(gb.at[c, pl.ds(0, 240)], ag_s.at[c], ag_r.at[c])

    def scatter_axis(c):
        core_in(c).wait_recv()
        own = cb[c, rows_at(core * 1024, 1024), :].astype(F32)
        b1[c] = (own + rc0[c].astype(F32)).astype(BF16).reshape(64, 16, 128)
        for copy in axis_copies(c, False, False):
            copy.start()

    def scatter_plane(c):
        a, q = place_in(c)
        for copy in axis_copies(c, False, True):
            copy.wait_recv()
        own = b1[c, pl.ds(a * 16, 16)].astype(F32)
        for d in range(3):
            own = own + ra[c, d].astype(F32)
        r1[c] = own.astype(BF16)
        rs[c, q] = r1[c, q]
        to_plane(c, False)

    def gather_plane(c):
        plane_scattered(c).wait_recv()
        gb[c, piece(c), :] = jnp.sum(rs[c, 0:16].astype(F32), 0).astype(BF16)
        to_plane(c, True)

    def gather_axis(c):
        plane_gathered(c).wait_recv()
        for copy in axis_copies(c, True, False):
            copy.start()

    def share_axis(c):
        for copy in axis_copies(c, True, True):
            copy.wait_recv()
        core_out(c, False).start()

    def out_copy(c):
        return pltpu.make_async_copy(gb.at[c], out_sum.at[c], out_sem.at[1 + c])

    def finish(c):
        core_out(c, True).wait_recv()
        out_copy(c).start()

    low = lax.broadcasted_iota(jnp.int32, (NT, 128), 1) < 64
    zero = jnp.zeros((), BF16)

    def by_head(x):
        return jnp.concatenate([jnp.where(low, x, zero), jnp.where(low, zero, x)], 0)

    def part_of(p, s):
        return pl.ds(pl.multiple_of(p * 384 + 128 * s, 128), 128)

    def forward(p, w):
        rows = slice(w * NT, w * NT + NT)
        s = dot_nt(qkv[rows, part_of(p, 1)], by_head(qkv[rows, part_of(p, 0)] * 0.125)) + bias_t[p]
        if w > 0:
            s = s + masks[w - 1]
        e = jnp.exp(s - jnp.max(s, 0, keepdims=True))
        prob = e * (1.0 / jnp.sum(e, 0, keepdims=True))
        probs[p, w] = prob
        both = dot(qkv[rows, part_of(p, 2)].T, prob.astype(BF16))
        att = jnp.concatenate([both[0:64, 0:NT], both[64:128, NT : 2 * NT]], 0)
        atts[w, pl.ds(pl.multiple_of(p * 128, 128), 128), :] = att.astype(BF16)

    def backward(p, w):
        rows = slice(w * NT, w * NT + NT)
        q2 = by_head(qkv[rows, part_of(p, 0)] * 0.125)
        ga2 = by_head(gatt[rows, pl.ds(pl.multiple_of(p * 128, 128), 128)])
        prob = probs[p, w]
        dp = dot_nt(qkv[rows, part_of(p, 2)], ga2)
        ds = prob * (dp - jnp.sum(prob * dp, 0, keepdims=True))
        if w == 0:
            dsum[p] = ds
        else:
            dsum[p] += ds
        db = ds.astype(BF16)
        dq = (dot(qkv[rows, part_of(p, 1)].T, db) * 0.125).astype(BF16).T
        dqkv[rows, part_of(p, 0)] = jnp.where(low, dq[0:NT], dq[NT : 2 * NT])
        dqkv[rows, part_of(p, 1)] = dot(db, q2).astype(BF16)
        dqkv[rows, part_of(p, 2)] = dot(prob.astype(BF16), ga2).astype(BF16)

    def forward_pair(p, _):
        for w in range(WINS):
            forward(p, w)
        return 0

    lax.fori_loop(0, PAIRS, forward_pair, 0)

    for copy in loads[14:]:
        copy.wait()
    for copy in gs:
        copy.wait_recv()
    spread_rows(gw)
    for w in range(WINS):
        gwin[w * NT : w * NT + NT, :] = window_rows(w).astype(BF16)

    def project_g(n, _):
        cols = pl.ds(pl.multiple_of(n * 256, 256), 256)
        gatt[:, cols] = dot_nt(gwin[...], wproj[cols, :]).astype(BF16)
        return 0

    lax.fori_loop(0, 2, project_g, 0)

    dproj = dot(atts[0], gwin[0:NT, :])
    for w in range(1, WINS):
        dproj = dproj + dot(atts[w], gwin[w * NT : w * NT + NT, :])
    for n in range(4):
        cb[0, 512 * n : 512 * n + 512, :] = dproj[:, 128 * n : 128 * n + 128].astype(BF16)
    chunk_done(0)

    def pair(p, _):
        for w in range(WINS):
            backward(p, w)
            if w == WINS - 1:
                cols = pl.ds(pl.multiple_of(p * 384, 128), 384)
                grads = dot(normt[...], dqkv[:, cols])
                for s in range(3):
                    block = 3 * p + s
                    cb[1 + block // 4, rows_at(block % 4 * 512, 512), :] = grads[:, 128 * s : 128 * s + 128].astype(BF16)

                @pl.when(p >= 1)
                def _():
                    chunk_done(p)

                part = dot_nt(dqkv[:, cols], wp[:, cols])

                @pl.when(p == 0)
                def _():
                    dn[...] = part

                @pl.when(p > 0)
                def _():
                    dn[...] += part

            for c, at, step in STEPS:
                if at % 4 == w:
                    call = {"axis": scatter_axis, "plane": scatter_plane}[step]
                    pl.when(p == at // 4)(functools.partial(call, c))
        return 0

    lax.fori_loop(0, PAIRS, pair, 0)

    for h in range(HEADS):
        one = dsum[h // 2, :, NT * (h % 2) : NT * (h % 2) + NT]
        one = jnp.concatenate([one, jnp.zeros((NT, 256 - NT), F32)], 1)
        for n in range(2):
            bj.at[n][pl.ds(h, NT, stride=8), :] = one[:, 128 * n : 128 * n + 128]
    sh[...] = dot(jnp.concatenate([bj[0], bj[1]], 1), picks((256, 384), 1), lax.Precision.HIGHEST)
    total = jnp.zeros((HEADS, 768), F32)
    rest = jnp.zeros((HEADS, 384), F32)
    for j in range(NT):
        at = place_of(j)
        wide = jnp.concatenate([sh[8 * j : 8 * j + 8, :], rest], 1)
        total = total + (wide if at == 0 else pltpu.roll(wide, at, 1))
    for n in range(6):
        exb[8 * n : 8 * n + 8, :] = total[:, 128 * n : 128 * n + 128]
    dg = jnp.zeros((1, D), F32)
    db = jnp.zeros((1, D), F32)
    for w in range(WINS):
        rows = slice(w * NT, w * NT + NT)
        d = dn[rows, :]
        dg = dg + jnp.sum(d * x32[rows, :], 0, keepdims=True)
        db = db + jnp.sum(d, 0, keepdims=True)
    for n in range(4):
        exb[48 + n : 49 + n, :] = dg[:, 128 * n : 128 * n + 128]
        exb[52 + n : 53 + n, :] = db[:, 128 * n : 128 * n + 128]

    def small(k, src, dst, device):
        return pltpu.make_async_remote_copy(
            src_ref=src, dst_ref=dst, send_sem=exs.at[k], recv_sem=exr.at[k],
            device_id=device, device_id_type=MESH,
        )

    def small_ring(axis, at, buf, k, arriving):
        src = buf.at[at]
        out = []
        for d in (1, 2, 3):
            dst = buf.at[turned(at, 4 - d, 4) if arriving else at]
            out.append(small(k + d - 1, src, dst, peer(axis, d)))
        return out

    def small_step(axis, at, buf, k):
        for copy in small_ring(axis, at, buf, k, True):
            copy.wait_recv()
        return (buf[0] + buf[1]) + (buf[2] + buf[3])

    first = small(0, exb, exc, other)
    first.start()
    scatter(3)
    gather_plane(0)
    scatter_plane(1)

    for w in range(WINS):
        rows = slice(w * NT, w * NT + NT)
        hat = x32[rows, :]
        g = dn[rows, :] * gain
        m1 = jnp.mean(g, -1, keepdims=True)
        m2 = jnp.mean(g * hat, -1, keepdims=True)
        branch = inv[rows, :] * (g - m1 - hat * m2)
        for k in range(2):
            for n in range(4):
                t32.at[n][level_rows(w, k), :] = branch[72 * k : 72 * k + 72, 128 * n : 128 * n + 128]
    for block in range(2):
        for half in range(2):
            at = (2 * block + half) * NT
            part = jnp.concatenate([t32[n, at : at + NT, :] for n in range(4)], 1)
            yw[block, half] = part.reshape(6, 6, 4, D).astype(BF16)

    def homeward(k, piece):
        rows, cols, at, dlat, dlon = piece
        return pltpu.make_async_remote_copy(
            src_ref=window_part(yw, at),
            dst_ref=grid_part(ret, rows, cols),
            send_sem=ret_s.at[k],
            recv_sem=ret_r.at[k],
            device_id=beside(-dlat, -dlon),
            device_id_type=MESH,
        )

    rets = [homeward(k, piece) for k, piece in enumerate(PIECES)]
    for copy in rets:
        copy.start()
    kept = []
    for k, (rows, cols, at) in enumerate(KEPT):
        kept.append(pltpu.make_async_copy(window_part(yw, at), grid_part(ret, rows, cols), load_sem.at[k]))
        kept[-1].start()

    scatter_plane(2)
    first.wait_recv()
    exx[xx] = exb[...] + exc[...]
    for copy in small_ring("x", xx, exx, 1, False):
        copy.start()
    gather_plane(1)
    gather_axis(0)
    gather_plane(2)
    exy[yy] = small_step("x", xx, exx, 1)
    for copy in small_ring("y", yy, exy, 4, False):
        copy.start()
    gather(3)

    for copy in kept:
        copy.wait()
    for copy in rets:
        copy.wait_recv()
    gnat[...] = (gnat[...].astype(F32) + ret[...].astype(F32)).astype(BF16)
    token_copy = pltpu.make_async_copy(gnat, out_tok, out_sem.at[0])
    token_copy.start()

    share_axis(0)
    gather_axis(1)
    gather_axis(2)
    exz[zz] = small_step("y", yy, exy, 4)
    for copy in small_ring("z", zz, exz, 7, False):
        copy.start()
    finish(0)
    share(3)
    share_axis(1)
    share_axis(2)
    finish(3)
    out_small[...] = small_step("z", zz, exz, 7) * FACTOR
    finish(1)
    finish(2)

    for copy in gs + rets + [first]:
        copy.wait_send()
    for axis, at, buf, k in (("x", xx, exx, 1), ("y", yy, exy, 4), ("z", zz, exz, 7)):
        for copy in small_ring(axis, at, buf, k, False):
            copy.wait_send()
    for c in range(PAIRS):
        core_in(c).wait_send()
        if c == 3:
            all_scattered(c).wait_send()
            all_gathered(c).wait_send()
        else:
            plane_scattered(c).wait_send()
            plane_gathered(c).wait_send()
            for copy in axis_copies(c, False, False) + axis_copies(c, True, False):
                copy.wait_send()
        core_out(c, False).wait_send()
        out_copy(c).wait()
    token_copy.wait()


def finish_kernel(tok_in, sum_hbm, small, out_tok, out_wqkv, out_wproj, out_gain, out_beta, out_table, gb, ow, op, tok, sems):
    tokens_in = pltpu.make_async_copy(tok_in, tok, sems.at[0])
    tokens = pltpu.make_async_copy(tok, out_tok, sems.at[1])
    loads = []
    for k in range(16):
        part = pl.ds(512 * (k % 4), 512)
        loads.append(pltpu.make_async_copy(sum_hbm.at[k // 4, part], gb.at[k // 4, part], sems.at[2 + k]))
    for k in range(16):
        loads[k].start()
        if k == 7:
            tokens_in.start()
    outs = []
    for k in range(16):
        loads[k].wait()
        part = gb[k // 4, 512 * (k % 4) : 512 * (k % 4) + 512, :].astype(F32) * FACTOR
        if k < 4:
            op[:, 128 * k : 128 * k + 128] = part
            cols = slice(128 * k, 128 * k + 128)
            outs.append(pltpu.make_async_copy(op.at[:, cols], out_wproj.at[:, cols], sems.at[18 + k]))
        else:
            pair, kind = divmod(k - 4, 3)
            cols = slice(512 * kind + 128 * pair, 512 * kind + 128 * pair + 128)
            ow[:, cols] = part
            outs.append(pltpu.make_async_copy(ow.at[:, cols], out_wqkv.at[:, cols], sems.at[18 + k]))
        outs[-1].start()
        if k == 11:
            tokens_in.wait()
            tokens.start()
    for n in range(5):
        out_table[:, 128 * n : 128 * n + 128] = small[8 * n : 8 * n + 8, :]
    out_table[:, 640:RELS] = small[40:48, 0 : RELS - 640]
    for n in range(4):
        out_gain[:, 128 * n : 128 * n + 128] = small[48 + n : 49 + n, :]
        out_beta[:, 128 * n : 128 * n + 128] = small[52 + n : 53 + n, :]
    for copy in outs + [tokens]:
        copy.wait()


def shards(tokens, grad_output, norm_gain, norm_bias, w_qkv, w_proj, rel_bias):
    any_space = pl.BlockSpec(memory_space=pl.ANY)
    vmem = pl.BlockSpec(memory_space=pltpu.VMEM)
    dma = pltpu.SemaphoreType.DMA
    by_window = (2, 2, 6, 6, 4, D)
    by_grid = (12, 12, 4, D)
    scratch = [
        pltpu.VMEM(by_window, BF16),
        pltpu.VMEM(by_window, BF16),
        pltpu.VMEM(by_grid, BF16),
        pltpu.VMEM(by_window, BF16),
        pltpu.VMEM(by_grid, BF16),
        pltpu.VMEM((D, 3 * D), BF16),
        pltpu.VMEM((D, D), BF16),
        pltpu.VMEM((TOK, D), F32),
        pltpu.VMEM((4, TOK, 128), F32),
        pltpu.VMEM((TOK, 1), F32),
        pltpu.VMEM((TOK, D), BF16),
        pltpu.VMEM((D, TOK), BF16),
        pltpu.VMEM((TOK, 3 * D), BF16),
        pltpu.VMEM((TOK, D), BF16),
        pltpu.VMEM((TOK, D), BF16),
        pltpu.VMEM((TOK, 3 * D), BF16),
        pltpu.VMEM((TOK, D), F32),
        pltpu.VMEM((HEADS, 768), F32),
        pltpu.VMEM((HEADS * NT, 384), F32),
        pltpu.VMEM((2, HEADS * NT, 128), F32),
        pltpu.VMEM((PAIRS, NT, 2 * NT), F32),
        pltpu.VMEM((3, NT, 2 * NT), F32),
        pltpu.VMEM((PAIRS, NT, 2 * NT), F32),
        pltpu.VMEM((PAIRS, WINS, NT, 2 * NT), F32),
        pltpu.VMEM((WINS, D, NT), BF16),
        pltpu.VMEM((PAIRS, 2048, 128), BF16),
        pltpu.VMEM((PAIRS, 1024, 128), BF16),
        pltpu.VMEM((PAIRS, 64, 16, 128), BF16),
        pltpu.VMEM((3, 3, 16, 16, 128), BF16),
        pltpu.VMEM((3, 16, 16, 128), BF16),
        pltpu.VMEM((PAIRS, 64, 16, 128), BF16),
        pltpu.VMEM((PAIRS, 2048, 128), BF16),
        pltpu.VMEM((56, 128), F32),
        pltpu.VMEM((56, 128), F32),
        pltpu.VMEM((4, 56, 128), F32),
        pltpu.VMEM((4, 56, 128), F32),
        pltpu.VMEM((4, 56, 128), F32),
        dma((18,)),
        dma((8,)),
        dma((8,)),
        dma((4,)),
        dma((4,)),
        dma((PAIRS, 2)),
        dma((PAIRS, 2)),
        dma((3, 6)),
        dma((3, 6)),
        dma((PAIRS,)),
        dma((PAIRS,)),
        dma((PAIRS,)),
        dma((PAIRS,)),
        dma((10,)),
        dma((10,)),
        dma((5,)),
    ]
    tok_out, summed, small = pl.pallas_call(
        kernel,
        out_shape=(
            jax.ShapeDtypeStruct(by_grid, BF16),
            jax.ShapeDtypeStruct((PAIRS, 2048, 128), BF16),
            jax.ShapeDtypeStruct((56, 128), F32),
        ),
        in_specs=[any_space, any_space, vmem, vmem, any_space, any_space, vmem],
        out_specs=(any_space, any_space, vmem),
        scratch_shapes=scratch,
        compiler_params=pltpu.CompilerParams(
            collective_id=0, has_side_effects=True, vmem_limit_bytes=56 * 1024 * 1024
        ),
    )(
        tokens.transpose(1, 2, 0, 3),
        grad_output.transpose(1, 2, 0, 3),
        norm_gain[None],
        norm_bias[None],
        w_qkv,
        w_proj,
        rel_bias,
    )
    out = pl.pallas_call(
        finish_kernel,
        out_shape=(
            jax.ShapeDtypeStruct(by_grid, BF16),
            jax.ShapeDtypeStruct((D, 3 * D), F32),
            jax.ShapeDtypeStruct((D, D), F32),
            jax.ShapeDtypeStruct((1, D), F32),
            jax.ShapeDtypeStruct((1, D), F32),
            jax.ShapeDtypeStruct((HEADS, RELS), F32),
        ),
        in_specs=[any_space, any_space, vmem],
        out_specs=(any_space, any_space, any_space, vmem, vmem, vmem),
        scratch_shapes=[
            pltpu.VMEM((PAIRS, 2048, 128), BF16),
            pltpu.VMEM((D, 3 * D), F32),
            pltpu.VMEM((D, D), F32),
            pltpu.VMEM(by_grid, BF16),
            dma((34,)),
        ],
        compiler_params=pltpu.CompilerParams(vmem_limit_bytes=60 * 1024 * 1024),
    )(tok_out, summed, small)
    return out[0].transpose(2, 0, 1, 3), out[1], out[2], out[3][0], out[4][0], out[5]


def solution(mesh):
    grid = P(None, "lat", "lon", None)
    return jax.shard_map(
        shards,
        mesh=mesh,
        in_specs=(grid, grid, P(), P(), P(), P(), P()),
        out_specs=(grid, P(), P(), P(), P(), P()),
        check_vma=False,
    )
```
